32 devices in a mesh: dp: 4 (over x, core), tm: 4 (over z), rows: 2 (over y).
Axes of the slice: x: 2, y: 2, z: 4, core: 2. Of those that a mesh axis runs over, the one named last changes fastest.
Arguments:
- latents: bfloat16 [4, 8, 2, 30, 512], P('dp', 'tm', 'rows'), may hold values from -6 to 6
- grad_out: bfloat16 [4, 8, 4, 60, 256], P('dp', 'tm', 'rows'), may hold values from -6 to 6
- kernel: bfloat16 [3, 3, 3, 512, 256], replicated, may hold values from -0.0546875 to 0.0546875
Outputs:
- grad_latents: bfloat16 [4, 8, 2, 30, 512], P('dp', 'tm', 'rows')
- weight_grad: float32 [512, 3, 3, 3, 256], P(('dp', 'tm', 'rows'))
The draws below stay inside these ranges and needn't reach their ends.
All inputs are finite; a program needn't handle non-finite values.
Results may differ from the reference program's by a relative error of at most 0.001.
Values may be sent and summed in bfloat16 or wider, within the bound.
No kernel may reach another device: no remote copies, remote signals or barrier semaphores. Data moves between devices by JAX's collectives and lax.ppermute only.
A program may use at most 128 MiB of HBM per device.

```python
import jax
import jax.numpy as jnp
from jax import lax

CIN = 512
COUT = 256
WL = 30
CLIPS = 4
FRAMES = 8
HL = 2
HUP = 4
WUP = 60


def with_spikes(values, stream_key, source, target, blocks, factor):
    owner, partner = [(jnp.arange(values.shape[axis_at]) // (values.shape[axis_at] // blocks)).reshape([-1 if axis == axis_at else 1 for axis in range(values.ndim)]) for axis_at in (source, target)]
    chosen = jax.random.permutation(stream_key, blocks)[partner]
    strong = (owner == chosen) | (owner == (partner + blocks // 2) % blocks)
    return jnp.where(strong, factor * values, values)


def block_scale(own_key, shape, shards, least, top_value):
    level, own = 1.0, jax.random.fold_in(own_key, 6)
    for dim, blocks in shards:
        draws = jnp.exp(jax.random.uniform(jax.random.fold_in(own, dim), (blocks,), jnp.float32, least / len(shards), top_value / len(shards)))
        level = level * jnp.repeat(draws, shape[dim] // blocks).reshape([-1 if axis == dim else 1 for axis in range(len(shape))])
    return level


def bell_draw(key, dims, deviation, reach, split=(), held_as=jnp.bfloat16):
    entries = deviation * jax.random.normal(key, dims, jnp.float32)
    if split:
        entries = entries * block_scale(key, dims, split, -0.22, 0.18)
    return jnp.clip(entries, -reach, reach).astype(held_as)


def heavy_noise(own_key, extent, spread, reach, cuts, heavy, dtype=jnp.bfloat16):
    result = spread * jax.random.normal(own_key, extent, jnp.float32)
    if cuts:
        result = result * block_scale(own_key, extent, cuts, -0.22, 0.18)
    return jnp.clip(with_spikes(result, jax.random.fold_in(own_key, 3), *heavy), -reach, reach).astype(dtype)


def setup_inputs(seed: int = 0) -> dict:
    streams_of = jax.random.split(jax.random.key(seed), 4)
    return {
        "latents": heavy_noise(streams_of[0], (CLIPS, FRAMES, HL, WL, CIN), 1.0, 6.0, ((0, 4), (1, 4), (2, 2)), (2, 4, 2, 2.0)),
        "grad_out": bell_draw(streams_of[1], (CLIPS, FRAMES, HUP, WUP, COUT), 1.0, 6.0, ((0, 4), (1, 4), (2, 2))),
        "kernel": bell_draw(streams_of[2], (3, 3, 3, CIN, COUT), (27 * CIN) ** -0.5, 0.0546875),
    }


def reference(latents, grad_out, kernel):
    frames = grad_out.shape[1]
    height = grad_out.shape[2]
    width = grad_out.shape[3]
    count = grad_out.shape[0] * frames * height * width
    factor = float(count) ** -0.5
    kernel_full = kernel.astype(jnp.float32)

    def one_clip(pair):
        clip, grad = pair
        grad_full = grad.astype(jnp.float32)
        upsampled = jnp.repeat(jnp.repeat(clip.astype(jnp.float32), 2, axis=1), 2, axis=2)
        up_pad = jnp.pad(upsampled, ((2, 0), (1, 1), (1, 1), (0, 0)))
        grad_pad = jnp.pad(grad_full, ((0, 2), (1, 1), (1, 1), (0, 0)))
        grad_up = jnp.zeros(upsampled.shape, jnp.float32)
        taps = []
        for a in range(3):
            for i in range(3):
                for j in range(3):
                    window = grad_pad[2 - a:2 - a + frames, 2 - i:2 - i + height, 2 - j:2 - j + width]
                    grad_up = grad_up + jnp.einsum("fhwo,co->fhwc", window, kernel_full[a, i, j], precision=lax.Precision.HIGHEST)
                    source = up_pad[a:a + frames, i:i + height, j:j + width]
                    taps.append(jnp.einsum("fhwc,fhwo->co", source, grad_full, precision=lax.Precision.HIGHEST))
        channels = grad_up.shape[3]
        pooled = grad_up.reshape(frames, height // 2, 2, width // 2, 2, channels).sum(axis=(2, 4))
        return pooled.astype(jnp.bfloat16), jnp.stack(taps, axis=1)

    grad_latents, terms = lax.map(one_clip, (latents, grad_out))
    summed = jnp.sum(terms, axis=0) * factor
    weight_grad = summed.reshape(summed.shape[0], 3, 3, 3, summed.shape[2])
    return grad_latents, weight_grad
```

```python
import functools

import jax
import jax.numpy as jnp
from jax import lax
from jax.experimental import pallas as pl
from jax.experimental.pallas import tpu as pltpu
from jax.sharding import PartitionSpec as P

VMEM_LIMIT = 40 * 1024 * 1024
SLOTS = (1, 3, 0, 2)


def cycle(size, by):
    return [(i, (i + by) % size) for i in range(size)]


def whole(count):
    return [pl.BlockSpec(memory_space=pltpu.VMEM)] * count


def params():
    return pltpu.CompilerParams(vmem_limit_bytes=VMEM_LIMIT)


def select_kernel(tm, share, lat_ref, own_ref, other_ref):
    channels = lat_ref.shape[1]
    width = channels // 2
    me_dp, me_tm, me_rows = lax.axis_index("dp"), lax.axis_index("tm"), lax.axis_index("rows")
    col = lax.broadcasted_iota(jnp.int32, (1, width), 1)
    inner = col % share
    place = (col // share) % 4
    shift = col // (4 * share)
    slot = jnp.where(place == 0, SLOTS[0], jnp.where(place == 1, SLOTS[1], jnp.where(place == 2, SLOTS[2], SLOTS[3])))
    dp = jnp.bitwise_xor(slot, me_dp)
    frame = (shift + me_tm) % tm
    row = lax.broadcasted_iota(jnp.int32, (channels, width), 0)
    for ref, rows in ((own_ref, me_rows), (other_ref, 1 - me_rows)):
        wanted = ((dp * tm + frame) * 2 + rows) * share + inner
        pick = jnp.where(row == wanted, 1.0, 0.0).astype(jnp.bfloat16)
        ref[...] = jnp.dot(lat_ref[...], pick, preferred_element_type=jnp.float32).astype(jnp.bfloat16)


def pair_kernel(tm, own_ref, other_ref, *outs):
    width = own_ref.shape[1] // tm
    for k in range(tm):
        cols = slice(k * width, (k + 1) * width)
        outs[k][...] = jnp.concatenate([own_ref[:, cols], other_ref[:, cols]], axis=1)


def windows_kernel(tm, share, *refs):
    pieces, out_ref, lat_ref, pick_ref = refs[:tm], refs[tm], refs[tm + 1], refs[tm + 2]
    group = 4 * share
    me_tm, me_rows = lax.axis_index("tm"), lax.axis_index("rows")
    lat_ref[...] = jnp.zeros_like(lat_ref)
    for k in range(tm):
        t = lax.rem(me_tm + tm - k, tm)
        block = pieces[k][...].astype(jnp.float32)
        lat_ref[t, me_rows, 0:60, :] = block[:, :group]
        lat_ref[t, 1 - me_rows, 0:60, :] = block[:, group:]
    kappa = lax.broadcasted_iota(jnp.int32, (128, 128), 0)
    rho = lax.broadcasted_iota(jnp.int32, (1, 128), 1)
    w, h = rho // 2, rho % 2
    for f in range(2):
        for ij in range(9):
            i, j = ij // 3, ij % 3
            for s in range(2):
                r = (2 * s + h + 1 + i) // 2 - 1
                q = (w + 1 + j) // 2 - 1
                ok = (r >= 0) & (r < 2) & (q >= 0) & (q < 30) & (rho < 120)
                target = jnp.where(ok, r * 64 + q * 2 + f, -1)
                pick = jnp.where(kappa == target, 1.0, 0.0).astype(jnp.bfloat16)
                base = (f * 9 + ij) * 256 + s * 128
                pick_ref[:, base : base + 128] = pick
    stacked = jnp.concatenate(
        [jnp.transpose(lat_ref[t].reshape(128, group)) for t in range(tm)], axis=0
    ).astype(jnp.bfloat16)
    out_ref[0:2] = jnp.zeros((2,) + out_ref.shape[1:], jnp.bfloat16)
    for f in range(2):
        for ij in range(9):
            base = (f * 9 + ij) * 256
            wide = jnp.dot(stacked, pick_ref[:, base : base + 256], preferred_element_type=jnp.float32)
            wide = wide.astype(jnp.bfloat16)
            for t in range(tm):
                for p in range(4):
                    src = t * group + p * share
                    dst = p * 9 * share + ij * share
                    out_ref[2 * t + f + 2, dst : dst + share, :] = wide[src : src + share]


def gather_kernel(tm, *refs):
    blocks, out_ref = refs[: 2 * tm], refs[2 * tm]
    me_tm, me_rows = lax.axis_index("tm"), lax.axis_index("rows")
    out_ref[:, :, 112:128, :] = jnp.zeros(out_ref.shape[:2] + (16, out_ref.shape[3]), jnp.bfloat16)
    for k in range(tm):
        t = lax.rem(me_tm + tm - k, tm)
        for f in range(2):
            out_ref[2 * t + f, me_rows, 0:120, :] = blocks[2 * k][f]
            out_ref[2 * t + f, 1 - me_rows, 0:120, :] = blocks[2 * k + 1][f]


def terms_kernel(a, frames, win_ref, grad_ref, send_ref, keep_ref):
    half = send_ref.shape[0]
    for ref, start in ((send_ref, 0), (keep_ref, half)):
        total = None
        for f in range(frames):
            g = grad_ref[f].reshape(256, grad_ref.shape[3])
            term = jnp.dot(win_ref[f + a, start : start + half, :], g, preferred_element_type=jnp.float32)
            total = term if total is None else total + term
        ref[...] = total


def latents_kernel(tm, own_ref, other_ref, next_ref, next_other_ref, kernel_ref, out_ref, wide_ref, pool_ref, total_ref):
    step = pl.program_id(0)
    outputs = own_ref.shape[2]

    @pl.when(step == 0)
    def _():
        me_tm, me_rows = lax.axis_index("tm"), lax.axis_index("rows")
        later = jnp.where(me_tm < tm - 1, 1.0, 0.0)
        above = jnp.where(me_rows > 0, 1.0, 0.0)
        lanes = outputs // 128
        wide_ref[:, :, 120:128, :] = jnp.zeros((2, lanes, 8, 128), jnp.float32)

        def every_fourth(source, first):
            parts = [wide_ref[source, n, pl.ds(first, 32, stride=4), :] for n in range(lanes)]
            return jnp.concatenate(parts, axis=1)

        for f in range(4):
            mine, theirs = (own_ref, other_ref) if f < 2 else (next_ref, next_other_ref)
            for n in range(lanes):
                wide_ref[0, n, 0:120, :] = mine[f % 2, :, 128 * n : 128 * n + 128].astype(jnp.float32)
                wide_ref[1, n, 0:120, :] = theirs[f % 2, :, 128 * n : 128 * n + 128].astype(jnp.float32)
            x = [[every_fourth(0, 2 * t + h) for t in range(2)] for h in range(2)]
            up = [every_fourth(1, 2 * t + 1) * above for t in range(2)]
            down = [every_fourth(1, 2 * t) * (1.0 - above) for t in range(2)]
            sums = (
                [x[1][t] + down[t] for t in range(2)],
                [x[0][t] + x[1][t] for t in range(2)],
                [up[t] + x[0][t] for t in range(2)],
            )
            for i in range(3):
                even, odd = sums[i]
                after = pltpu.roll(even, 31, 0)
                before = pltpu.roll(odd, 1, 0)
                for j, pooled in enumerate((odd + after, even + odd, before + even)):
                    if f >= 2:
                        pooled = pooled * later
                    high = pooled.astype(jnp.bfloat16)
                    low = (pooled - high.astype(jnp.float32)).astype(jnp.bfloat16)
                    pool_ref[3 * i + j, 0, f] = high
                    pool_ref[3 * i + j, 1, f] = low
        total_ref[...] = jnp.zeros_like(total_ref)

    total = total_ref[...]
    for ij in range(9):
        lhs = pool_ref[ij, :, pl.ds(2 - step, 2)].reshape(128, outputs)
        total = total + lax.dot_general(
            lhs, kernel_ref[ij], (((1,), (1,)), ((), ())), preferred_element_type=jnp.float32
        )
    total_ref[...] = total

    @pl.when(step == 2)
    def _():
        for f in range(2):
            sum_f = total[32 * f : 32 * f + 32] + total[64 + 32 * f : 96 + 32 * f]
            out_ref[f] = sum_f[0:30].astype(jnp.bfloat16)


def narrow_body(latents, grad_out, kernel):
    tm = lax.axis_size("tm")
    devices = lax.axis_size("dp") * tm * 2
    channels = latents.shape[4]
    outputs = grad_out.shape[4]
    share = channels // devices
    frames = 2 * tm
    factor = float(devices * 240) ** (-0.5)
    swap = [(0, 1), (1, 0)]

    mine = jnp.transpose(grad_out[0], (0, 2, 1, 3)).reshape(2, 120, outputs)
    shifted = [mine] + [lax.ppermute(mine, "tm", cycle(tm, k)) for k in range(1, tm)]
    across = [lax.ppermute(block, "rows", swap) for block in shifted]

    lat = jnp.transpose(latents[0, :, 0], (1, 0, 2)).reshape(60, channels)
    half = jax.ShapeDtypeStruct((60, channels // 2), jnp.bfloat16)
    own, other = pl.pallas_call(
        functools.partial(select_kernel, tm, share),
        out_shape=(half, half),
        in_specs=whole(1),
        out_specs=tuple(whole(2)),
        compiler_params=params(),
    )(lat)
    other = lax.ppermute(other, "rows", swap)
    pieces = pl.pallas_call(
        functools.partial(pair_kernel, tm),
        out_shape=tuple([jax.ShapeDtypeStruct((60, 8 * share), jnp.bfloat16)] * tm),
        in_specs=whole(2),
        out_specs=tuple(whole(tm)),
        compiler_params=params(),
    )(own, other)
    pieces = [pieces[0]] + [lax.ppermute(pieces[k], "tm", cycle(tm, k)) for k in range(1, tm)]
    windows = pl.pallas_call(
        functools.partial(windows_kernel, tm, share),
        out_shape=jax.ShapeDtypeStruct((frames + 2, 36 * share, 256), jnp.bfloat16),
        in_specs=whole(tm),
        out_specs=whole(1)[0],
        scratch_shapes=[pltpu.VMEM((tm, 2, 64, 4 * share), jnp.float32), pltpu.VMEM((128, 18 * 256), jnp.bfloat16)],
        compiler_params=params(),
    )(*pieces)
    grads = pl.pallas_call(
        functools.partial(gather_kernel, tm),
        out_shape=jax.ShapeDtypeStruct((frames, 2, 128, outputs), jnp.bfloat16),
        in_specs=whole(2 * tm),
        out_specs=whole(1)[0],
        compiler_params=params(),
    )(*[block for pair in zip(shifted, across) for block in pair])

    rows = 18 * share
    parts = []
    for a in range(3):
        send, keep = pl.pallas_call(
            functools.partial(terms_kernel, a, frames),
            out_shape=tuple([jax.ShapeDtypeStruct((rows, outputs), jnp.float32)] * 2),
            in_specs=whole(2),
            out_specs=tuple(whole(2)),
            compiler_params=params(),
        )(windows, grads)
        both = keep + lax.ppermute(send, "dp", [(i, i ^ 1) for i in range(4)])
        kept, sent = both[: rows // 2], both[rows // 2 :]
        parts.append((kept + lax.ppermute(sent, "dp", [(i, i ^ 2) for i in range(4)])) * factor)
    weight_grad = jnp.stack(parts).reshape(3, 3, 3, share, outputs)
    weight_grad = jnp.transpose(weight_grad, (3, 0, 1, 2, 4))

    taps = kernel.reshape(27, channels, outputs)
    grad_latents = pl.pallas_call(
        functools.partial(latents_kernel, tm),
        grid=(3,),
        out_shape=jax.ShapeDtypeStruct((2, 30, channels), jnp.bfloat16),
        in_specs=[pl.BlockSpec((2, 120, outputs), lambda a: (0, 0, 0))] * 4
        + [pl.BlockSpec((9, channels, outputs), lambda a: (a, 0, 0))],
        out_specs=pl.BlockSpec((2, 30, channels), lambda a: (0, 0, 0)),
        scratch_shapes=[
            pltpu.VMEM((2, outputs // 128, 128, 128), jnp.float32),
            pltpu.VMEM((9, 2, 4, 32, outputs), jnp.bfloat16),
            pltpu.VMEM((128, channels), jnp.float32),
        ],
        compiler_params=params(),
    )(shifted[0], across[0], shifted[tm - 1], across[tm - 1], taps)
    return (grad_latents.reshape(latents.shape), weight_grad)


def from_behind(shard, axis, by):
    peers = lax.axis_size(axis)
    pairs = [(i, i + by) for i in range(peers) if 0 <= i + by < peers]
    return lax.ppermute(shard, axis, pairs)


def with_halo(block, sides, width):
    for axis, dim in sides:
        count = lax.axis_size(axis)
        forward = [(i, i + 1) for i in range(count - 1)]
        backward = [(target, source) for source, target in forward]
        low = lax.ppermute(
            lax.slice_in_dim(block, block.shape[dim] - width, None, axis=dim), axis, forward
        )
        high = lax.ppermute(lax.slice_in_dim(block, 0, width, axis=dim), axis, backward)
        block = jnp.concatenate([low, block, high], axis=dim)
    return block


def tap_terms(source, grad_flat, frames, height, width):
    taps = []
    for a in range(3):
        for i in range(3):
            for j in range(3):
                window = source[a : a + frames, i : i + height, j : j + width]
                flat = window.reshape(frames * height * width, window.shape[3])
                taps.append(
                    lax.dot_general(
                        flat,
                        grad_flat,
                        (((0,), (0,)), ((), ())),
                        preferred_element_type=jnp.float32,
                    )
                )
    return jnp.stack(taps, axis=1)


def wide_body(latents, grad_out, kernel):
    frames = grad_out.shape[1]
    height = grad_out.shape[2]
    width = grad_out.shape[3]
    channels = latents.shape[4]
    outputs = grad_out.shape[4]
    devices = lax.axis_size("dp") * lax.axis_size("tm") * lax.axis_size("rows")
    factor = float(devices * frames * height * width) ** (-0.5)
    earlier = from_behind(latents, "tm", 1)
    with_earlier = jnp.concatenate([earlier, latents], axis=1)
    grad_ext = with_halo(grad_out, (("rows", 2),), 1)
    later = from_behind(grad_ext, "tm", -1)
    grad_all = jnp.concatenate([grad_ext, later], axis=1)[0]
    grad_all = jnp.pad(grad_all, ((0, 0), (0, 0), (1, 1), (0, 0)))
    grad_up = jnp.zeros((frames, height, width, channels), jnp.float32)
    for a in range(3):
        for i in range(3):
            for j in range(3):
                window = grad_all[
                    2 - a : 2 - a + frames, 2 - i : 2 - i + height, 2 - j : 2 - j + width
                ]
                grad_up = grad_up + lax.dot_general(
                    window,
                    kernel[a, i, j],
                    (((3,), (1,)), ((), ())),
                    preferred_element_type=jnp.float32,
                )
    pooled = grad_up.reshape(frames, height // 2, 2, width // 2, 2, channels).sum(axis=(2, 4))
    grad_latents = pooled.astype(jnp.bfloat16)[None]
    slab_count = lax.axis_size("rows")
    groups = lax.axis_size("dp") * lax.axis_size("tm")
    share = channels // devices
    lead = with_earlier.shape[:4]
    regrouped = with_earlier.reshape(lead + (groups, slab_count, share))
    regrouped = jnp.swapaxes(regrouped, 4, 5).reshape(lead + (channels,))
    owned = lax.all_to_all(regrouped, "rows", split_axis=4, concat_axis=2, tiled=True)[0]
    source = jnp.repeat(jnp.repeat(owned, 2, axis=1), 2, axis=2)
    source = jnp.pad(source, ((0, 0), (1, 1), (1, 1), (0, 0)))
    grad_whole = lax.all_gather(grad_out, "rows", axis=2, tiled=True)[0]
    whole_height = grad_whole.shape[1]
    grad_flat = grad_whole.reshape(frames * whole_height * width, outputs)
    term = tap_terms(source, grad_flat, frames, whole_height, width) * factor
    term = term.reshape(source.shape[3], 3, 3, 3, outputs)
    weight_grad = lax.psum_scatter(term, ("dp", "tm"), scatter_dimension=0, tiled=True)
    return (grad_latents, weight_grad)


def body(latents, grad_out, kernel):
    share = latents.shape[4] // (lax.axis_size("dp") * lax.axis_size("tm") * lax.axis_size("rows"))
    narrow = lax.axis_size("rows") == 2 and lax.axis_size("dp") == 4 and share % 16 == 0
    return (narrow_body if narrow else wide_body)(latents, grad_out, kernel)


def solution(mesh):
    in_specs = (P("dp", "tm", "rows", None, None), P("dp", "tm", "rows", None, None), P())
    out_specs = (P("dp", "tm", "rows", None, None), P(("dp", "tm", "rows"), None, None, None, None))
    return jax.shard_map(body, mesh=mesh, in_specs=in_specs, out_specs=out_specs, check_vma=False)
```

```python
import functools

import jax
import jax.numpy as jnp
from jax import lax
from jax.experimental import pallas as pl
from jax.experimental.pallas import tpu as pltpu
from jax.sharding import PartitionSpec as P

VMEM_LIMIT = 40 * 1024 * 1024
SLOTS = (3, 2, 1, 0)


def cycle(size, by):
    return [(i, (i + by) % size) for i in range(size)]


def whole(count):
    return [pl.BlockSpec(memory_space=pltpu.VMEM)] * count


def params(limit=VMEM_LIMIT):
    return pltpu.CompilerParams(vmem_limit_bytes=limit)


def light():
    return pl.CostEstimate(flops=1, bytes_accessed=1, transcendentals=0)


LATENT_ROWS = 16
MESSAGE_ROWS = LATENT_ROWS + 120


def message_kernel(tm, share, lat_ref, grad_ref, *refs):
    outs, wide_ref = refs[:tm], refs[tm]
    channels = lat_ref.shape[1]
    me_dp, me_tm, me_rows = lax.axis_index("dp"), lax.axis_index("tm"), lax.axis_index("rows")
    col = lax.broadcasted_iota(jnp.int32, (1, channels), 1)
    inner = col % share
    place = (col // share) % 4
    crossing = (col // (4 * share)) % 2
    shift = col // (8 * share)
    slot = jnp.where(place == 0, SLOTS[0], jnp.where(place == 1, SLOTS[1], jnp.where(place == 2, SLOTS[2], SLOTS[3])))
    dp = jnp.bitwise_xor(slot, me_dp)
    rows = jnp.bitwise_xor(crossing, me_rows)
    wanted = ((dp * tm + (shift + me_tm) % tm) * 2 + rows) * share + inner
    row = lax.broadcasted_iota(jnp.int32, (channels, channels), 0)
    pick = jnp.where(row == wanted, 1.0, 0.0).astype(jnp.bfloat16)
    wide_ref[48:64, :] = jnp.zeros((16, channels), jnp.float32)
    wide_ref[0:60, :] = jnp.dot(lat_ref[...], pick, preferred_element_type=jnp.float32)
    for k in range(tm):
        for part in range(4):
            piece = wide_ref[16 * part : 16 * part + 16, 128 * k : 128 * k + 128]
            lanes = slice(128 * (part % 2), 128 * (part % 2) + 128)
            outs[k][part // 2, 0:LATENT_ROWS, lanes] = piece.astype(jnp.bfloat16)
        for f in range(2):
            outs[k][f, LATENT_ROWS:, :] = grad_ref[f]


def arrange_kernel(tm, share, shifts, *refs):
    blocks = refs[: 2 * len(shifts)]
    win_ref, grad_ref, pick_ref, lat_ref = refs[-4:]
    group = 4 * share
    me_tm, me_rows = lax.axis_index("tm"), lax.axis_index("rows")
    if 0 in shifts:
        kappa = lax.broadcasted_iota(jnp.int32, (128, 128), 0)
        rho = lax.broadcasted_iota(jnp.int32, (1, 128), 1)
        w, h = rho // 2, rho % 2
        for f in range(2):
            for ij in range(9):
                i, j = ij // 3, ij % 3
                for s in range(2):
                    r = (2 * s + h + 1 + i) // 2 - 1
                    q = (w + 1 + j) // 2 - 1
                    ok = (r >= 0) & (r < 2) & (q >= 0) & (q < 30) & (rho < 120)
                    target = jnp.where(ok, r * 64 + q * 2 + f, -1)
                    pick = jnp.where(kappa == target, 1.0, 0.0).astype(jnp.bfloat16)
                    base = (f * 9 + ij) * 256 + s * 128
                    pick_ref[:, base : base + 128] = pick
        win_ref[0:2] = jnp.zeros((2,) + win_ref.shape[1:], jnp.bfloat16)
    where = [lax.rem(me_tm + tm - k, tm) for k in shifts]
    for n, t in enumerate(where):
        for half, rows in enumerate((me_rows, 1 - me_rows)):
            block = blocks[2 * n + half]
            for part in range(4):
                lanes = 128 * (part % 2) + group * half
                piece = block[part // 2, 0:LATENT_ROWS, lanes : lanes + group]
                lat_ref[n, rows, 16 * part : 16 * part + 16, :] = piece.astype(jnp.float32)
            for f in range(2):
                grad_ref[2 * t + f, rows, 112:128, :] = jnp.zeros((16, grad_ref.shape[3]), jnp.bfloat16)
                grad_ref[2 * t + f, rows, 0:120, :] = block[f, LATENT_ROWS:, :]
    stacked = jnp.concatenate(
        [jnp.transpose(lat_ref[n].reshape(128, group)) for n in range(len(shifts))], axis=0
    ).astype(jnp.bfloat16)
    for f in range(2):
        for ij in range(9):
            base = (f * 9 + ij) * 256
            wide = jnp.dot(stacked, pick_ref[:, base : base + 256], preferred_element_type=jnp.float32)
            wide = wide.astype(jnp.bfloat16)
            for n, t in enumerate(where):
                for p in range(4):
                    src = n * group + p * share
                    dst = p * 9 * share + ij * share
                    win_ref[2 * t + f + 2, dst : dst + share, :] = wide[src : src + share]


def terms_kernel(first, taps, frames, win_ref, grad_ref, send_ref, keep_ref):
    rows = send_ref.shape[0] // len(taps)
    for n, a in enumerate(taps):
        for ref, start in ((send_ref, first), (keep_ref, first + rows)):
            total = None
            for f in range(frames):
                g = grad_ref[f].reshape(256, grad_ref.shape[3])
                term = jnp.dot(win_ref[f + a, start : start + rows, :], g, preferred_element_type=jnp.float32)
                total = term if total is None else total + term
            ref[n * rows : (n + 1) * rows] = total


def latents_kernel(tm, own_ref, other_ref, next_ref, next_other_ref, kernel_ref, out_ref, wide_ref, pool_ref, total_ref):
    step = pl.program_id(0)
    outputs = own_ref.shape[2]

    @pl.when(step == 0)
    def _():
        me_tm, me_rows = lax.axis_index("tm"), lax.axis_index("rows")
        later = jnp.where(me_tm < tm - 1, 1.0, 0.0)
        above = jnp.where(me_rows > 0, 1.0, 0.0)
        lanes = outputs // 128
        wide_ref[:, :, 120:128, :] = jnp.zeros((2, lanes, 8, 128), jnp.float32)

        def every_fourth(source, first):
            parts = [wide_ref[source, n, pl.ds(first, 32, stride=4), :] for n in range(lanes)]
            return jnp.concatenate(parts, axis=1)

        for f in range(4):
            mine, theirs = (own_ref, other_ref) if f < 2 else (next_ref, next_other_ref)
            for n in range(lanes):
                wide_ref[0, n, 0:120, :] = mine[f % 2, LATENT_ROWS:, 128 * n : 128 * n + 128].astype(jnp.float32)
                wide_ref[1, n, 0:120, :] = theirs[f % 2, LATENT_ROWS:, 128 * n : 128 * n + 128].astype(jnp.float32)
            x = [[every_fourth(0, 2 * t + h) for t in range(2)] for h in range(2)]
            up = [every_fourth(1, 2 * t + 1) * above for t in range(2)]
            down = [every_fourth(1, 2 * t) * (1.0 - above) for t in range(2)]
            sums = (
                [x[1][t] + down[t] for t in range(2)],
                [x[0][t] + x[1][t] for t in range(2)],
                [up[t] + x[0][t] for t in range(2)],
            )
            for i in range(3):
                even, odd = sums[i]
                after = pltpu.roll(even, 31, 0)
                before = pltpu.roll(odd, 1, 0)
                for j, pooled in enumerate((odd + after, even + odd, before + even)):
                    if f >= 2:
                        pooled = pooled * later
                    high = pooled.astype(jnp.bfloat16)
                    low = (pooled - high.astype(jnp.float32)).astype(jnp.bfloat16)
                    pool_ref[3 * i + j, 0, f] = high
                    pool_ref[3 * i + j, 1, f] = low
        total_ref[...] = jnp.zeros_like(total_ref)

    total = total_ref[...]
    for ij in range(9):
        lhs = pool_ref[ij, :, pl.ds(2 - step, 2)].reshape(128, outputs)
        total = total + lax.dot_general(
            lhs, kernel_ref[ij], (((1,), (1,)), ((), ())), preferred_element_type=jnp.float32
        )
    total_ref[...] = total

    @pl.when(step == 2)
    def _():
        for f in range(2):
            sum_f = total[32 * f : 32 * f + 32] + total[64 + 32 * f : 96 + 32 * f]
            out_ref[f] = sum_f[0:30].astype(jnp.bfloat16)


def narrow_body(latents, grad_out, kernel):
    tm = lax.axis_size("tm")
    devices = lax.axis_size("dp") * tm * 2
    channels = latents.shape[4]
    outputs = grad_out.shape[4]
    share = channels // devices
    frames = 2 * tm
    factor = float(devices * 240) ** (-0.5)
    swap = [(0, 1), (1, 0)]

    mine = jnp.transpose(grad_out[0], (0, 2, 1, 3)).reshape(2, 120, outputs)
    lat = jnp.transpose(latents[0, :, 0], (1, 0, 2)).reshape(60, channels)
    message = jax.ShapeDtypeStruct((2, MESSAGE_ROWS, outputs), jnp.bfloat16)
    messages = pl.pallas_call(
        functools.partial(message_kernel, tm, share),
        out_shape=tuple([message] * tm),
        in_specs=whole(2),
        out_specs=tuple(whole(tm)),
        scratch_shapes=[pltpu.VMEM((64, channels), jnp.float32)],
        compiler_params=params(),
    )(lat, mine)
    order = [0, tm - 1] + list(range(1, tm - 1))
    shifted = {k: lax.ppermute(messages[k], "tm", cycle(tm, k)) if k else messages[0] for k in order}
    across = {k: lax.ppermute(shifted[k], "rows", swap) for k in order}

    arranged = (
        jax.ShapeDtypeStruct((frames + 2, 36 * share, 256), jnp.bfloat16),
        jax.ShapeDtypeStruct((frames, 2, 128, outputs), jnp.bfloat16),
        jax.ShapeDtypeStruct((128, 18 * 256), jnp.bfloat16),
    )

    def arrange(shifts, earlier):
        blocks = [block for k in shifts for block in (shifted[k], across[k])]
        return pl.pallas_call(
            functools.partial(arrange_kernel, tm, share, tuple(shifts)),
            out_shape=arranged,
            in_specs=whole(len(blocks) + len(earlier)),
            out_specs=tuple(whole(3)),
            scratch_shapes=[pltpu.VMEM((len(shifts), 2, 64, 4 * share), jnp.float32)],
            input_output_aliases={len(blocks) + n: n for n in range(len(earlier))},
            compiler_params=params(),
        )(*blocks, *earlier)

    early = arrange(order[:-1], ())
    windows, grads, _ = arrange(order[-1:], early)

    rows = 9 * share

    def terms(first, taps, windows):
        return pl.pallas_call(
            functools.partial(terms_kernel, first, taps, frames),
            out_shape=tuple([jax.ShapeDtypeStruct((len(taps) * rows, outputs), jnp.float32)] * 2),
            in_specs=whole(2),
            out_specs=tuple(whole(2)),
            compiler_params=params(),
            cost_estimate=light(),
        )(windows, grads)

    def other_core(block):
        return lax.ppermute(block, "dp", [(i, i ^ 1) for i in range(4)])

    send, keep = terms(0, (0, 1, 2), windows)
    chip = keep + other_core(send)
    crossed = lax.ppermute(chip, "dp", [(i, i ^ 2) for i in range(4)])
    windows, first, *_ = lax.optimization_barrier((windows, shifted[0], chip))
    taps = kernel.reshape(27, channels, outputs)
    grad_latents = pl.pallas_call(
        functools.partial(latents_kernel, tm),
        grid=(3,),
        out_shape=jax.ShapeDtypeStruct((2, 30, channels), jnp.bfloat16),
        in_specs=[pl.BlockSpec((2, MESSAGE_ROWS, outputs), lambda a: (0, 0, 0))] * 4
        + [pl.BlockSpec((9, channels, outputs), lambda a: (a, 0, 0))],
        out_specs=pl.BlockSpec((2, 30, channels), lambda a: (0, 0, 0)),
        scratch_shapes=[
            pltpu.VMEM((2, outputs // 128, 128, 128), jnp.float32),
            pltpu.VMEM((9, 2, 4, 32, outputs), jnp.bfloat16),
            pltpu.VMEM((128, channels), jnp.float32),
        ],
        compiler_params=params(),
        cost_estimate=light(),
    )(first, across[0], shifted[tm - 1], across[tm - 1], taps)

    stay = []
    for a in range(3):
        send, keep = terms(2 * rows, (a,), windows)
        stay.append(keep + other_core(send))
    total = (jnp.concatenate(stay) + crossed) * factor
    weight_grad = jnp.transpose(total.reshape(3, 3, 3, share, outputs), (3, 0, 1, 2, 4))
    return (grad_latents.reshape(latents.shape), weight_grad)


def from_behind(shard, axis, by):
    peers = lax.axis_size(axis)
    pairs = [(i, i + by) for i in range(peers) if 0 <= i + by < peers]
    return lax.ppermute(shard, axis, pairs)


def with_halo(block, sides, width):
    for axis, dim in sides:
        count = lax.axis_size(axis)
        forward = [(i, i + 1) for i in range(count - 1)]
        backward = [(target, source) for source, target in forward]
        low = lax.ppermute(
            lax.slice_in_dim(block, block.shape[dim] - width, None, axis=dim), axis, forward
        )
        high = lax.ppermute(lax.slice_in_dim(block, 0, width, axis=dim), axis, backward)
        block = jnp.concatenate([low, block, high], axis=dim)
    return block


def tap_terms(source, grad_flat, frames, height, width):
    taps = []
    for a in range(3):
        for i in range(3):
            for j in range(3):
                window = source[a : a + frames, i : i + height, j : j + width]
                flat = window.reshape(frames * height * width, window.shape[3])
                taps.append(
                    lax.dot_general(
                        flat,
                        grad_flat,
                        (((0,), (0,)), ((), ())),
                        preferred_element_type=jnp.float32,
                    )
                )
    return jnp.stack(taps, axis=1)


def wide_body(latents, grad_out, kernel):
    frames = grad_out.shape[1]
    height = grad_out.shape[2]
    width = grad_out.shape[3]
    channels = latents.shape[4]
    outputs = grad_out.shape[4]
    devices = lax.axis_size("dp") * lax.axis_size("tm") * lax.axis_size("rows")
    factor = float(devices * frames * height * width) ** (-0.5)
    earlier = from_behind(latents, "tm", 1)
    with_earlier = jnp.concatenate([earlier, latents], axis=1)
    grad_ext = with_halo(grad_out, (("rows", 2),), 1)
    later = from_behind(grad_ext, "tm", -1)
    grad_all = jnp.concatenate([grad_ext, later], axis=1)[0]
    grad_all = jnp.pad(grad_all, ((0, 0), (0, 0), (1, 1), (0, 0)))
    grad_up = jnp.zeros((frames, height, width, channels), jnp.float32)
    for a in range(3):
        for i in range(3):
            for j in range(3):
                window = grad_all[
                    2 - a : 2 - a + frames, 2 - i : 2 - i + height, 2 - j : 2 - j + width
                ]
                grad_up = grad_up + lax.dot_general(
                    window,
                    kernel[a, i, j],
                    (((3,), (1,)), ((), ())),
                    preferred_element_type=jnp.float32,
                )
    pooled = grad_up.reshape(frames, height // 2, 2, width // 2, 2, channels).sum(axis=(2, 4))
    grad_latents = pooled.astype(jnp.bfloat16)[None]
    slab_count = lax.axis_size("rows")
    groups = lax.axis_size("dp") * lax.axis_size("tm")
    share = channels // devices
    lead = with_earlier.shape[:4]
    regrouped = with_earlier.reshape(lead + (groups, slab_count, share))
    regrouped = jnp.swapaxes(regrouped, 4, 5).reshape(lead + (channels,))
    owned = lax.all_to_all(regrouped, "rows", split_axis=4, concat_axis=2, tiled=True)[0]
    source = jnp.repeat(jnp.repeat(owned, 2, axis=1), 2, axis=2)
    source = jnp.pad(source, ((0, 0), (1, 1), (1, 1), (0, 0)))
    grad_whole = lax.all_gather(grad_out, "rows", axis=2, tiled=True)[0]
    whole_height = grad_whole.shape[1]
    grad_flat = grad_whole.reshape(frames * whole_height * width, outputs)
    term = tap_terms(source, grad_flat, frames, whole_height, width) * factor
    term = term.reshape(source.shape[3], 3, 3, 3, outputs)
    weight_grad = lax.psum_scatter(term, ("dp", "tm"), scatter_dimension=0, tiled=True)
    return (grad_latents, weight_grad)


def body(latents, grad_out, kernel):
    share = latents.shape[4] // (lax.axis_size("dp") * lax.axis_size("tm") * lax.axis_size("rows"))
    narrow = lax.axis_size("rows") == 2 and lax.axis_size("dp") == 4 and share == 16
    return (narrow_body if narrow else wide_body)(latents, grad_out, kernel)


def solution(mesh):
    in_specs = (P("dp", "tm", "rows", None, None), P("dp", "tm", "rows", None, None), P())
    out_specs = (P("dp", "tm", "rows", None, None), P(("dp", "tm", "rows"), None, None, None, None))
    return jax.shard_map(body, mesh=mesh, in_specs=in_specs, out_specs=out_specs, check_vma=False)
```

```python
import functools

import jax
import jax.numpy as jnp
from jax import lax
from jax.experimental import pallas as pl
from jax.experimental.pallas import tpu as pltpu
from jax.sharding import PartitionSpec as P

VMEM_LIMIT = 40 * 1024 * 1024
SLOTS = (3, 2, 1, 0)


def cycle(size, by):
    return [(i, (i + by) % size) for i in range(size)]


def whole(count):
    return [pl.BlockSpec(memory_space=pltpu.VMEM)] * count


def params(limit=VMEM_LIMIT):
    return pltpu.CompilerParams(vmem_limit_bytes=limit)


def light():
    return pl.CostEstimate(flops=1, bytes_accessed=1, transcendentals=0)


LATENT_ROWS = 16
MESSAGE_ROWS = LATENT_ROWS + 120


def select_kernel(tm, share, lat_ref, wide_ref):
    channels = lat_ref.shape[2]
    me_dp, me_tm, me_rows = lax.axis_index("dp"), lax.axis_index("tm"), lax.axis_index("rows")
    col = lax.broadcasted_iota(jnp.int32, (1, channels), 1)
    inner = col % share
    place = (col // share) % 4
    crossing = (col // (4 * share)) % 2
    shift = col // (8 * share)
    slot = jnp.where(place == 0, SLOTS[0], jnp.where(place == 1, SLOTS[1], jnp.where(place == 2, SLOTS[2], SLOTS[3])))
    dp = jnp.bitwise_xor(slot, me_dp)
    rows = jnp.bitwise_xor(crossing, me_rows)
    wanted = ((dp * tm + (shift + me_tm) % tm) * 2 + rows) * share + inner
    row = lax.broadcasted_iota(jnp.int32, (channels, channels), 0)
    pick = jnp.where(row == wanted, 1.0, 0.0).astype(jnp.bfloat16)
    wide_ref[56:64, :] = jnp.zeros((8, channels), jnp.float32)
    wide_ref[0:60, :] = jnp.dot(lat_ref[...].reshape(60, channels), pick, preferred_element_type=jnp.float32)


def message_kernel(tm, wide_ref, grad_ref, *outs):
    grads = [grad_ref[f].reshape(120, grad_ref.shape[3]) for f in range(2)]
    for k in range(tm):
        for part in range(4):
            piece = wide_ref[16 * part : 16 * part + 16, 128 * k : 128 * k + 128].astype(jnp.bfloat16)
            lanes = slice(128 * (part % 2), 128 * (part % 2) + 128)
            outs[k][part // 2, 0:LATENT_ROWS, lanes] = piece
        for f in range(2):
            outs[k][f, LATENT_ROWS:, :] = grads[f]


def arrange_kernel(tm, share, shifts, *refs):
    blocks = refs[: 2 * len(shifts)]
    win_ref, grad_ref, pick_ref, lat_ref = refs[-4:]
    group = 4 * share
    me_tm, me_rows = lax.axis_index("tm"), lax.axis_index("rows")
    if 0 in shifts:
        kappa = lax.broadcasted_iota(jnp.int32, (128, 128), 0)
        rho = lax.broadcasted_iota(jnp.int32, (1, 128), 1)
        w, h = rho // 2, rho % 2
        for f in range(2):
            for ij in range(9):
                i, j = ij // 3, ij % 3
                for s in range(2):
                    r = (2 * s + h + 1 + i) // 2 - 1
                    q = (w + 1 + j) // 2 - 1
                    ok = (r >= 0) & (r < 2) & (q >= 0) & (q < 30) & (rho < 120)
                    target = jnp.where(ok, r * 64 + q * 2 + f, -1)
                    pick = jnp.where(kappa == target, 1.0, 0.0).astype(jnp.bfloat16)
                    base = (f * 9 + ij) * 256 + s * 128
                    pick_ref[:, base : base + 128] = pick
        win_ref[0:2] = jnp.zeros((2,) + win_ref.shape[1:], jnp.bfloat16)
    where = [lax.rem(me_tm + tm - k, tm) for k in shifts]
    for n, t in enumerate(where):
        for half, rows in enumerate((me_rows, 1 - me_rows)):
            block = blocks[2 * n + half]
            for part in range(4):
                lanes = slice(128 * (part % 2) + group * half, 128 * (part % 2) + group * (half + 1))
                piece = block[part // 2, 0:LATENT_ROWS, lanes]
                lat_ref[n, rows, 16 * part : 16 * part + 16, :] = piece.astype(jnp.float32)
            for f in range(2):
                grad_ref[2 * t + f, rows, 112:128, :] = jnp.zeros((16, grad_ref.shape[3]), jnp.bfloat16)
                grad_ref[2 * t + f, rows, 0:120, :] = block[f, LATENT_ROWS:, :]
    stacked = jnp.concatenate(
        [jnp.transpose(lat_ref[n].reshape(128, group)) for n in range(len(shifts))], axis=0
    ).astype(jnp.bfloat16)
    for f in range(2):
        for ij in range(9):
            base = (f * 9 + ij) * 256
            wide = jnp.dot(stacked, pick_ref[:, base : base + 256], preferred_element_type=jnp.float32)
            wide = wide.astype(jnp.bfloat16)
            for n, t in enumerate(where):
                for p in range(4):
                    src = n * group + p * share
                    dst = p * 9 * share + ij * share
                    win_ref[2 * t + f + 2, dst : dst + share, :] = wide[src : src + share]


def terms_kernel(first, taps, frames, outs, win_ref, grad_ref, *out_refs):
    each = len(out_refs) // outs
    rows = out_refs[0].shape[0] * each // len(taps)
    span = slice(first, first + rows * outs)
    total = None
    for f in range(frames):
        grad = grad_ref[f].reshape(256, grad_ref.shape[3])
        lhs = jnp.concatenate([win_ref[f + a, span, :] for a in taps], axis=0)
        term = jnp.dot(lhs, grad, preferred_element_type=jnp.float32)
        total = term if total is None else total + term
    for n in range(len(taps)):
        for m in range(outs):
            start = (n * outs + m) * rows
            ref = out_refs[m * each + n % each]
            place = n // each * rows
            ref[place : place + rows] = total[start : start + rows]


TOP_EXPONENT = 14
EXPONENT_ROWS = 16


def pack_kernel(keep_ref, received_ref, out_ref):
    rows = keep_ref.shape[0]
    total = keep_ref[...] + received_ref[...]
    top = jnp.max(jnp.max(jnp.abs(total), axis=0, keepdims=True), axis=1, keepdims=True)
    exponent = jnp.floor(jnp.log2(jnp.maximum(top, 2.0**-100))) - TOP_EXPONENT
    out_ref[0:rows] = total * jnp.exp2(-exponent)
    out_ref[rows:] = jnp.broadcast_to(exponent, (EXPONENT_ROWS, out_ref.shape[1]))


def latents_kernel(tm, own_ref, other_ref, next_ref, next_other_ref, kernel_ref, out_ref, wide_ref, pool_ref, total_ref):
    step = pl.program_id(0)
    outputs = own_ref.shape[2]

    @pl.when(step == 0)
    def _():
        me_tm, me_rows = lax.axis_index("tm"), lax.axis_index("rows")
        later = jnp.where(me_tm < tm - 1, 1.0, 0.0)
        above = jnp.where(me_rows > 0, 1.0, 0.0)
        lanes = outputs // 128
        wide_ref[:, :, 120:128, :] = jnp.zeros((2, lanes, 8, 128), jnp.float32)

        def every_fourth(source, first):
            parts = [wide_ref[source, n, pl.ds(first, 32, stride=4), :] for n in range(lanes)]
            return jnp.concatenate(parts, axis=1)

        for f in range(4):
            mine, theirs = (own_ref, other_ref) if f < 2 else (next_ref, next_other_ref)
            for n in range(lanes):
                wide_ref[0, n, 0:120, :] = mine[f % 2, LATENT_ROWS:, 128 * n : 128 * n + 128].astype(jnp.float32)
                wide_ref[1, n, 0:120, :] = theirs[f % 2, LATENT_ROWS:, 128 * n : 128 * n + 128].astype(jnp.float32)
            x = [[every_fourth(0, 2 * t + h) for t in range(2)] for h in range(2)]
            up = [every_fourth(1, 2 * t + 1) * above for t in range(2)]
            down = [every_fourth(1, 2 * t) * (1.0 - above) for t in range(2)]
            sums = (
                [x[1][t] + down[t] for t in range(2)],
                [x[0][t] + x[1][t] for t in range(2)],
                [up[t] + x[0][t] for t in range(2)],
            )
            for i in range(3):
                even, odd = sums[i]
                after = pltpu.roll(even, 31, 0)
                before = pltpu.roll(odd, 1, 0)
                for j, pooled in enumerate((odd + after, even + odd, before + even)):
                    if f >= 2:
                        pooled = pooled * later
                    high = pooled.astype(jnp.bfloat16)
                    low = (pooled - high.astype(jnp.float32)).astype(jnp.bfloat16)
                    pool_ref[3 * i + j, 0, f] = high
                    pool_ref[3 * i + j, 1, f] = low
        total_ref[...] = jnp.zeros_like(total_ref)

    total = total_ref[...]
    for ij in range(9):
        lhs = pool_ref[ij, :, pl.ds(2 - step, 2)].reshape(128, outputs)
        total = total + lax.dot_general(
            lhs, kernel_ref[ij], (((1,), (1,)), ((), ())), preferred_element_type=jnp.float32
        )
    total_ref[...] = total

    @pl.when(step == 2)
    def _():
        for f in range(2):
            sum_f = total[32 * f : 32 * f + 32] + total[64 + 32 * f : 96 + 32 * f]
            out_ref[f] = sum_f[0:30].astype(jnp.bfloat16)


def narrow_body(latents, grad_out, kernel):
    tm = lax.axis_size("tm")
    devices = lax.axis_size("dp") * tm * 2
    channels = latents.shape[4]
    outputs = grad_out.shape[4]
    share = channels // devices
    frames = 2 * tm
    factor = float(devices * 240) ** (-0.5)
    swap = [(0, 1), (1, 0)]

    mine = jnp.transpose(grad_out[0], (0, 2, 1, 3))
    lat = jnp.transpose(latents[0, :, 0], (1, 0, 2))
    message = jax.ShapeDtypeStruct((2, MESSAGE_ROWS, outputs), jnp.bfloat16)
    selected = pl.pallas_call(
        functools.partial(select_kernel, tm, share),
        out_shape=jax.ShapeDtypeStruct((64, channels), jnp.float32),
        in_specs=whole(1),
        out_specs=whole(1)[0],
        compiler_params=params(),
    )(lat)
    messages = pl.pallas_call(
        functools.partial(message_kernel, tm),
        out_shape=tuple([message] * tm),
        in_specs=whole(2),
        out_specs=tuple(whole(tm)),
        compiler_params=params(),
    )(selected, mine)
    order = [0, tm - 1] + list(range(1, tm - 1))
    shifted = [lax.ppermute(messages[k], "tm", cycle(tm, k)) if k else messages[0] for k in order]
    across = [lax.ppermute(block, "rows", swap) for block in shifted]

    arranged = (
        jax.ShapeDtypeStruct((frames + 2, 36 * share, 256), jnp.bfloat16),
        jax.ShapeDtypeStruct((frames, 2, 128, outputs), jnp.bfloat16),
        jax.ShapeDtypeStruct((128, 18 * 256), jnp.bfloat16),
    )

    def arrange(first, last, earlier):
        blocks = [block for n in range(first, last) for block in (shifted[n], across[n])]
        return pl.pallas_call(
            functools.partial(arrange_kernel, tm, share, tuple(order[first:last])),
            out_shape=arranged,
            in_specs=whole(len(blocks) + len(earlier)),
            out_specs=tuple(whole(3)),
            scratch_shapes=[pltpu.VMEM((last - first, 2, 64, 4 * share), jnp.float32)],
            input_output_aliases={len(blocks) + n: n for n in range(len(earlier))},
            compiler_params=params(),
            cost_estimate=light(),
        )(*blocks, *earlier)

    early = arrange(0, tm - 1, ())
    windows, grads, _ = arrange(tm - 1, tm, early)

    rows = 9 * share

    def terms(first, windows, outs, each):
        out = jax.ShapeDtypeStruct((3 // each * rows, outputs), jnp.float32)
        return pl.pallas_call(
            functools.partial(terms_kernel, first, (0, 1, 2), frames, outs),
            out_shape=tuple([out] * (outs * each)),
            in_specs=whole(2),
            out_specs=tuple(whole(outs * each)),
            compiler_params=params(),
            cost_estimate=light(),
        )(windows, grads)

    def other_core(block):
        return lax.ppermute(block, "dp", [(i, i ^ 1) for i in range(4)])

    (send,) = terms(0, windows, 1, 1)
    after, _ = lax.optimization_barrier((windows, send))
    (keep,) = terms(rows, after, 1, 1)
    chip = pl.pallas_call(
        pack_kernel,
        out_shape=jax.ShapeDtypeStruct((3 * rows + EXPONENT_ROWS, outputs), jnp.float32),
        in_specs=whole(2),
        out_specs=whole(1)[0],
        compiler_params=params(),
        cost_estimate=light(),
    )(keep, other_core(send))
    chip = chip.astype(jnp.float16)
    crossed = lax.ppermute(chip, "dp", [(i, i ^ 2) for i in range(4)]).astype(jnp.float32)
    crossed = crossed[: 3 * rows] * (jnp.exp2(crossed[3 * rows : 3 * rows + 1]) * factor)
    windows, first, *_ = lax.optimization_barrier((windows, shifted[0], chip))
    taps = kernel.reshape(27, channels, outputs)
    grad_latents = pl.pallas_call(
        functools.partial(latents_kernel, tm),
        grid=(3,),
        out_shape=jax.ShapeDtypeStruct((2, 30, channels), jnp.bfloat16),
        in_specs=[pl.BlockSpec((2, MESSAGE_ROWS, outputs), lambda a: (0, 0, 0))] * 4
        + [pl.BlockSpec((9, channels, outputs), lambda a: (a, 0, 0))],
        out_specs=pl.BlockSpec((2, 30, channels), lambda a: (0, 0, 0)),
        scratch_shapes=[
            pltpu.VMEM((2, outputs // 128, 128, 128), jnp.float32),
            pltpu.VMEM((9, 2, 4, 32, outputs), jnp.bfloat16),
            pltpu.VMEM((128, channels), jnp.float32),
        ],
        compiler_params=params(),
        cost_estimate=light(),
    )(first, across[0], shifted[1], across[1], taps)

    parts = terms(2 * rows, windows, 2, 3)
    stay = [keep + other_core(send) for send, keep in zip(parts[:3], parts[3:])]
    total = jnp.concatenate(stay) * factor + crossed
    weight_grad = jnp.transpose(total.reshape(3, 3, 3, share, outputs), (3, 0, 1, 2, 4))
    return (grad_latents.reshape(latents.shape), weight_grad)


def from_behind(shard, axis, by):
    peers = lax.axis_size(axis)
    pairs = [(i, i + by) for i in range(peers) if 0 <= i + by < peers]
    return lax.ppermute(shard, axis, pairs)


def with_halo(block, sides, width):
    for axis, dim in sides:
        count = lax.axis_size(axis)
        forward = [(i, i + 1) for i in range(count - 1)]
        backward = [(target, source) for source, target in forward]
        low = lax.ppermute(
            lax.slice_in_dim(block, block.shape[dim] - width, None, axis=dim), axis, forward
        )
        high = lax.ppermute(lax.slice_in_dim(block, 0, width, axis=dim), axis, backward)
        block = jnp.concatenate([low, block, high], axis=dim)
    return block


def tap_terms(source, grad_flat, frames, height, width):
    taps = []
    for a in range(3):
        for i in range(3):
            for j in range(3):
                window = source[a : a + frames, i : i + height, j : j + width]
                flat = window.reshape(frames * height * width, window.shape[3])
                taps.append(
                    lax.dot_general(
                        flat,
                        grad_flat,
                        (((0,), (0,)), ((), ())),
                        preferred_element_type=jnp.float32,
                    )
                )
    return jnp.stack(taps, axis=1)


def wide_body(latents, grad_out, kernel):
    frames = grad_out.shape[1]
    height = grad_out.shape[2]
    width = grad_out.shape[3]
    channels = latents.shape[4]
    outputs = grad_out.shape[4]
    devices = lax.axis_size("dp") * lax.axis_size("tm") * lax.axis_size("rows")
    factor = float(devices * frames * height * width) ** (-0.5)
    earlier = from_behind(latents, "tm", 1)
    with_earlier = jnp.concatenate([earlier, latents], axis=1)
    grad_ext = with_halo(grad_out, (("rows", 2),), 1)
    later = from_behind(grad_ext, "tm", -1)
    grad_all = jnp.concatenate([grad_ext, later], axis=1)[0]
    grad_all = jnp.pad(grad_all, ((0, 0), (0, 0), (1, 1), (0, 0)))
    grad_up = jnp.zeros((frames, height, width, channels), jnp.float32)
    for a in range(3):
        for i in range(3):
            for j in range(3):
                window = grad_all[
                    2 - a : 2 - a + frames, 2 - i : 2 - i + height, 2 - j : 2 - j + width
                ]
                grad_up = grad_up + lax.dot_general(
                    window,
                    kernel[a, i, j],
                    (((3,), (1,)), ((), ())),
                    preferred_element_type=jnp.float32,
                )
    pooled = grad_up.reshape(frames, height // 2, 2, width // 2, 2, channels).sum(axis=(2, 4))
    grad_latents = pooled.astype(jnp.bfloat16)[None]
    slab_count = lax.axis_size("rows")
    groups = lax.axis_size("dp") * lax.axis_size("tm")
    share = channels // devices
    lead = with_earlier.shape[:4]
    regrouped = with_earlier.reshape(lead + (groups, slab_count, share))
    regrouped = jnp.swapaxes(regrouped, 4, 5).reshape(lead + (channels,))
    owned = lax.all_to_all(regrouped, "rows", split_axis=4, concat_axis=2, tiled=True)[0]
    source = jnp.repeat(jnp.repeat(owned, 2, axis=1), 2, axis=2)
    source = jnp.pad(source, ((0, 0), (1, 1), (1, 1), (0, 0)))
    grad_whole = lax.all_gather(grad_out, "rows", axis=2, tiled=True)[0]
    whole_height = grad_whole.shape[1]
    grad_flat = grad_whole.reshape(frames * whole_height * width, outputs)
    term = tap_terms(source, grad_flat, frames, whole_height, width) * factor
    term = term.reshape(source.shape[3], 3, 3, 3, outputs)
    weight_grad = lax.psum_scatter(term, ("dp", "tm"), scatter_dimension=0, tiled=True)
    return (grad_latents, weight_grad)


def body(latents, grad_out, kernel):
    share = latents.shape[4] // (lax.axis_size("dp") * lax.axis_size("tm") * lax.axis_size("rows"))
    narrow = lax.axis_size("rows") == 2 and lax.axis_size("dp") == 4 and lax.axis_size("tm") > 2 and share == 16
    return (narrow_body if narrow else wide_body)(latents, grad_out, kernel)


def solution(mesh):
    in_specs = (P("dp", "tm", "rows", None, None), P("dp", "tm", "rows", None, None), P())
    out_specs = (P("dp", "tm", "rows", None, None), P(("dp", "tm", "rows"), None, None, None, None))
    return jax.shard_map(body, mesh=mesh, in_specs=in_specs, out_specs=out_specs, check_vma=False)
```

```python
import functools

import jax
import jax.numpy as jnp
from jax import lax
from jax.experimental import pallas as pl
from jax.experimental.pallas import tpu as pltpu
from jax.sharding import PartitionSpec as P

VMEM_LIMIT = 40 * 1024 * 1024
SLOTS = (3, 2, 1, 0)


def cycle(size, by):
    return [(i, (i + by) % size) for i in range(size)]


def whole(count):
    return [pl.BlockSpec(memory_space=pltpu.VMEM)] * count


def params(limit=VMEM_LIMIT):
    return pltpu.CompilerParams(vmem_limit_bytes=limit)


def light():
    return pl.CostEstimate(flops=1, bytes_accessed=1, transcendentals=0)


LATENT_ROWS = 16
MESSAGE_ROWS = LATENT_ROWS + 120


def select_kernel(tm, share, lat_ref, wide_ref):
    channels = lat_ref.shape[2]
    me_dp, me_tm, me_rows = lax.axis_index("dp"), lax.axis_index("tm"), lax.axis_index("rows")
    col = lax.broadcasted_iota(jnp.int32, (1, channels), 1)
    inner = col % share
    place = (col // share) % 4
    crossing = (col // (4 * share)) % 2
    shift = col // (8 * share)
    slot = jnp.where(place == 0, SLOTS[0], jnp.where(place == 1, SLOTS[1], jnp.where(place == 2, SLOTS[2], SLOTS[3])))
    dp = jnp.bitwise_xor(slot, me_dp)
    rows = jnp.bitwise_xor(crossing, me_rows)
    wanted = ((dp * tm + (shift + me_tm) % tm) * 2 + rows) * share + inner
    row = lax.broadcasted_iota(jnp.int32, (channels, channels), 0)
    pick = jnp.where(row == wanted, 1.0, 0.0).astype(jnp.bfloat16)
    wide_ref[56:64, :] = jnp.zeros((8, channels), jnp.float32)
    wide_ref[0:60, :] = jnp.dot(lat_ref[...].reshape(60, channels), pick, preferred_element_type=jnp.float32)


def message_kernel(tm, wide_ref, grad_ref, *outs):
    grads = [grad_ref[f].reshape(120, grad_ref.shape[3]) for f in range(2)]
    for k in range(tm):
        for part in range(4):
            piece = wide_ref[16 * part : 16 * part + 16, 128 * k : 128 * k + 128].astype(jnp.bfloat16)
            lanes = slice(128 * (part % 2), 128 * (part % 2) + 128)
            outs[k][part // 2, 0:LATENT_ROWS, lanes] = piece
        for f in range(2):
            outs[k][f, LATENT_ROWS:, :] = grads[f]


def arrange_kernel(tm, share, shifts, late, *refs):
    blocks = refs[: 2 * len(shifts)]
    win_ref, grad_ref, pick_ref, lat_ref = refs[-4:]
    group = 4 * share
    me_tm, me_rows = lax.axis_index("tm"), lax.axis_index("rows")
    if 0 in shifts:
        kappa = lax.broadcasted_iota(jnp.int32, (128, 128), 0)
        rho = lax.broadcasted_iota(jnp.int32, (1, 128), 1)
        w, h = rho // 2, rho % 2
        for f in range(2):
            for ij in range(9):
                i, j = ij // 3, ij % 3
                for s in range(2):
                    r = (2 * s + h + 1 + i) // 2 - 1
                    q = (w + 1 + j) // 2 - 1
                    ok = (r >= 0) & (r < 2) & (q >= 0) & (q < 30) & (rho < 120)
                    target = jnp.where(ok, r * 64 + q * 2 + f, -1)
                    pick = jnp.where(kappa == target, 1.0, 0.0).astype(jnp.bfloat16)
                    base = (f * 9 + ij) * 256 + s * 128
                    pick_ref[:, base : base + 128] = pick
        win_ref[0:2] = jnp.zeros((2,) + win_ref.shape[1:], jnp.bfloat16)
        t = lax.rem(me_tm + tm - late, tm)
        win_ref[pl.ds(2 * t + 2, 2)] = jnp.zeros((2,) + win_ref.shape[1:], jnp.bfloat16)
        grad_ref[pl.ds(2 * t, 2)] = jnp.zeros((2,) + grad_ref.shape[1:], jnp.bfloat16)
    where = [lax.rem(me_tm + tm - k, tm) for k in shifts]
    for n, t in enumerate(where):
        for half, rows in enumerate((me_rows, 1 - me_rows)):
            block = blocks[2 * n + half]
            for part in range(4):
                lanes = slice(128 * (part % 2) + group * half, 128 * (part % 2) + group * (half + 1))
                piece = block[part // 2, 0:LATENT_ROWS, lanes]
                lat_ref[n, rows, 16 * part : 16 * part + 16, :] = piece.astype(jnp.float32)
            for f in range(2):
                grad_ref[2 * t + f, rows, 112:128, :] = jnp.zeros((16, grad_ref.shape[3]), jnp.bfloat16)
                grad_ref[2 * t + f, rows, 0:120, :] = block[f, LATENT_ROWS:, :]
    stacked = jnp.concatenate(
        [jnp.transpose(lat_ref[n].reshape(128, group)) for n in range(len(shifts))], axis=0
    ).astype(jnp.bfloat16)
    for f in range(2):
        for ij in range(9):
            base = (f * 9 + ij) * 256
            wide = jnp.dot(stacked, pick_ref[:, base : base + 256], preferred_element_type=jnp.float32)
            wide = wide.astype(jnp.bfloat16)
            for n, t in enumerate(where):
                for p in range(4):
                    src = n * group + p * share
                    dst = p * 9 * share + ij * share
                    win_ref[2 * t + f + 2, dst : dst + share, :] = wide[src : src + share]


def terms_kernel(first, taps, frames, outs, win_ref, grad_ref, *out_refs):
    each = len(out_refs) // outs
    rows = out_refs[0].shape[0] * each // len(taps)
    span = slice(first, first + rows * outs)
    total = None
    for f in range(frames):
        grad = grad_ref[f].reshape(256, grad_ref.shape[3])
        lhs = jnp.concatenate([win_ref[f + a, span, :] for a in taps], axis=0)
        term = jnp.dot(lhs, grad, preferred_element_type=jnp.float32)
        total = term if total is None else total + term
    for n in range(len(taps)):
        for m in range(outs):
            start = (n * outs + m) * rows
            ref = out_refs[m * each + n % each]
            place = n // each * rows
            ref[place : place + rows] = total[start : start + rows]


def late_terms(tm, late, first, win_ref, grad_ref, part_ref, out_ref):
    rows = part_ref.shape[0] // 3
    frames = grad_ref.shape[0]
    block = lax.rem(lax.axis_index("tm") + tm - late, tm)
    total = [part_ref[a * rows : (a + 1) * rows] for a in range(3)]
    for step, taps in enumerate(((0, 1, 2), (0, 1, 2), (0, 1), (0,))):
        frame = 2 * block + step
        if step > 1:
            inside = jnp.where(frame < frames, 1.0, 0.0).astype(jnp.bfloat16)
            frame = jnp.minimum(frame, frames - 1)
        grad = grad_ref[frame].reshape(256, grad_ref.shape[3])
        if step > 1:
            grad = grad * inside
        lhs = jnp.concatenate([win_ref[frame + a, first : first + rows, :] for a in taps], axis=0)
        term = jnp.dot(lhs, grad, preferred_element_type=jnp.float32)
        for n, a in enumerate(taps):
            total[a] = total[a] + term[n * rows : (n + 1) * rows]
    for a in range(3):
        out_ref[a * rows : (a + 1) * rows] = total[a]


def arrange_late_kernel(tm, share, late, own_ref, other_ref, w_ref, g_ref, p_ref, part_ref, *refs):
    win_ref, grad_ref, pick_ref, out_ref, lat_ref = refs
    arrange_kernel(tm, share, (late,), late, own_ref, other_ref, win_ref, grad_ref, pick_ref, lat_ref)
    late_terms(tm, late, 0, win_ref, grad_ref, part_ref, out_ref)


def keep_late_kernel(tm, late, win_ref, grad_ref, part_ref, out_ref):
    late_terms(tm, late, part_ref.shape[0] // 3, win_ref, grad_ref, part_ref, out_ref)


TOP_EXPONENT = 14
EXPONENT_ROWS = 16


def pack_kernel(keep_ref, received_ref, out_ref):
    rows = keep_ref.shape[0]
    total = keep_ref[...] + received_ref[...]
    top = jnp.max(jnp.max(jnp.abs(total), axis=0, keepdims=True), axis=1, keepdims=True)
    exponent = jnp.floor(jnp.log2(jnp.maximum(top, 2.0**-100))) - TOP_EXPONENT
    out_ref[0:rows] = total * jnp.exp2(-exponent)
    out_ref[rows:] = jnp.broadcast_to(exponent, (EXPONENT_ROWS, out_ref.shape[1]))


def latents_kernel(tm, own_ref, other_ref, next_ref, next_other_ref, kernel_ref, out_ref, wide_ref, pool_ref, total_ref):
    step = pl.program_id(0)
    outputs = own_ref.shape[2]

    @pl.when(step == 0)
    def _():
        me_tm, me_rows = lax.axis_index("tm"), lax.axis_index("rows")
        later = jnp.where(me_tm < tm - 1, 1.0, 0.0)
        above = jnp.where(me_rows > 0, 1.0, 0.0)
        lanes = outputs // 128
        wide_ref[:, :, 120:128, :] = jnp.zeros((2, lanes, 8, 128), jnp.float32)

        def every_fourth(source, first):
            parts = [wide_ref[source, n, pl.ds(first, 32, stride=4), :] for n in range(lanes)]
            return jnp.concatenate(parts, axis=1)

        for f in range(4):
            mine, theirs = (own_ref, other_ref) if f < 2 else (next_ref, next_other_ref)
            for n in range(lanes):
                wide_ref[0, n, 0:120, :] = mine[f % 2, LATENT_ROWS:, 128 * n : 128 * n + 128].astype(jnp.float32)
                wide_ref[1, n, 0:120, :] = theirs[f % 2, LATENT_ROWS:, 128 * n : 128 * n + 128].astype(jnp.float32)
            x = [[every_fourth(0, 2 * t + h) for t in range(2)] for h in range(2)]
            up = [every_fourth(1, 2 * t + 1) * above for t in range(2)]
            down = [every_fourth(1, 2 * t) * (1.0 - above) for t in range(2)]
            sums = (
                [x[1][t] + down[t] for t in range(2)],
                [x[0][t] + x[1][t] for t in range(2)],
                [up[t] + x[0][t] for t in range(2)],
            )
            for i in range(3):
                even, odd = sums[i]
                after = pltpu.roll(even, 31, 0)
                before = pltpu.roll(odd, 1, 0)
                for j, pooled in enumerate((odd + after, even + odd, before + even)):
                    if f >= 2:
                        pooled = pooled * later
                    high = pooled.astype(jnp.bfloat16)
                    low = (pooled - high.astype(jnp.float32)).astype(jnp.bfloat16)
                    pool_ref[3 * i + j, 0, f] = high
                    pool_ref[3 * i + j, 1, f] = low
        total_ref[...] = jnp.zeros_like(total_ref)

    total = total_ref[...]
    for ij in range(9):
        lhs = pool_ref[ij, :, pl.ds(2 - step, 2)].reshape(128, outputs)
        total = total + lax.dot_general(
            lhs, kernel_ref[ij], (((1,), (1,)), ((), ())), preferred_element_type=jnp.float32
        )
    total_ref[...] = total

    @pl.when(step == 2)
    def _():
        for f in range(2):
            sum_f = total[32 * f : 32 * f + 32] + total[64 + 32 * f : 96 + 32 * f]
            out_ref[f] = sum_f[0:30].astype(jnp.bfloat16)


def narrow_body(latents, grad_out, kernel):
    tm = lax.axis_size("tm")
    devices = lax.axis_size("dp") * tm * 2
    channels = latents.shape[4]
    outputs = grad_out.shape[4]
    share = channels // devices
    frames = 2 * tm
    factor = float(devices * 240) ** (-0.5)
    swap = [(0, 1), (1, 0)]

    mine = jnp.transpose(grad_out[0], (0, 2, 1, 3))
    lat = jnp.transpose(latents[0, :, 0], (1, 0, 2))
    message = jax.ShapeDtypeStruct((2, MESSAGE_ROWS, outputs), jnp.bfloat16)
    selected = pl.pallas_call(
        functools.partial(select_kernel, tm, share),
        out_shape=jax.ShapeDtypeStruct((64, channels), jnp.float32),
        in_specs=whole(1),
        out_specs=whole(1)[0],
        compiler_params=params(),
        cost_estimate=pl.CostEstimate(flops=2**31, bytes_accessed=2**24, transcendentals=0),
    )(lat)
    messages = pl.pallas_call(
        functools.partial(message_kernel, tm),
        out_shape=tuple([message] * tm),
        in_specs=whole(2),
        out_specs=tuple(whole(tm)),
        compiler_params=params(),
    )(selected, mine)
    order = [0, tm - 1] + list(range(1, tm - 1))
    shifted = [lax.ppermute(messages[k], "tm", cycle(tm, k)) if k else messages[0] for k in order]
    across = [lax.ppermute(block, "rows", swap) for block in shifted]

    arranged = (
        jax.ShapeDtypeStruct((frames + 2, 36 * share, 256), jnp.bfloat16),
        jax.ShapeDtypeStruct((frames, 2, 128, outputs), jnp.bfloat16),
        jax.ShapeDtypeStruct((128, 18 * 256), jnp.bfloat16),
    )

    late = order[-1]
    early = [block for pair in zip(shifted[:-1], across[:-1]) for block in pair]
    early = pl.pallas_call(
        functools.partial(arrange_kernel, tm, share, tuple(order[:-1]), late),
        out_shape=arranged,
        in_specs=whole(len(early)),
        out_specs=tuple(whole(3)),
        scratch_shapes=[pltpu.VMEM((tm - 1, 2, 64, 4 * share), jnp.float32)],
        compiler_params=params(),
        cost_estimate=light(),
    )(*early)

    rows = 9 * share

    def terms(first, windows, grads, outs, each):
        out = jax.ShapeDtypeStruct((3 // each * rows, outputs), jnp.float32)
        return pl.pallas_call(
            functools.partial(terms_kernel, first, (0, 1, 2), frames, outs),
            out_shape=tuple([out] * (outs * each)),
            in_specs=whole(2),
            out_specs=tuple(whole(outs * each)),
            compiler_params=params(),
            cost_estimate=light(),
        )(windows, grads)

    def other_core(block):
        return lax.ppermute(block, "dp", [(i, i ^ 1) for i in range(4)])

    send, keep = terms(0, early[0], early[1], 2, 1)
    windows, grads, _, send = pl.pallas_call(
        functools.partial(arrange_late_kernel, tm, share, late),
        out_shape=arranged + (jax.ShapeDtypeStruct(send.shape, jnp.float32),),
        in_specs=whole(6),
        out_specs=tuple(whole(4)),
        scratch_shapes=[pltpu.VMEM((1, 2, 64, 4 * share), jnp.float32)],
        input_output_aliases={2: 0, 3: 1, 4: 2},
        compiler_params=params(),
        cost_estimate=light(),
    )(shifted[-1], across[-1], *early, send)
    keep = pl.pallas_call(
        functools.partial(keep_late_kernel, tm, late),
        out_shape=jax.ShapeDtypeStruct(keep.shape, jnp.float32),
        in_specs=whole(3),
        out_specs=whole(1)[0],
        compiler_params=params(),
        cost_estimate=light(),
    )(windows, grads, keep)
    chip = pl.pallas_call(
        pack_kernel,
        out_shape=jax.ShapeDtypeStruct((3 * rows + EXPONENT_ROWS, outputs), jnp.float32),
        in_specs=whole(2),
        out_specs=whole(1)[0],
        compiler_params=params(),
        cost_estimate=light(),
    )(keep, other_core(send))
    chip = chip.astype(jnp.float16)
    crossed = lax.ppermute(chip, "dp", [(i, i ^ 2) for i in range(4)]).astype(jnp.float32)
    crossed = crossed[: 3 * rows] * (jnp.exp2(crossed[3 * rows : 3 * rows + 1]) * factor)
    windows, first, *_ = lax.optimization_barrier((windows, shifted[0], chip))
    taps = kernel.reshape(27, channels, outputs)
    grad_latents = pl.pallas_call(
        functools.partial(latents_kernel, tm),
        grid=(3,),
        out_shape=jax.ShapeDtypeStruct((2, 30, channels), jnp.bfloat16),
        in_specs=[pl.BlockSpec((2, MESSAGE_ROWS, outputs), lambda a: (0, 0, 0))] * 4
        + [pl.BlockSpec((9, channels, outputs), lambda a: (a, 0, 0))],
        out_specs=pl.BlockSpec((2, 30, channels), lambda a: (0, 0, 0)),
        scratch_shapes=[
            pltpu.VMEM((2, outputs // 128, 128, 128), jnp.float32),
            pltpu.VMEM((9, 2, 4, 32, outputs), jnp.bfloat16),
            pltpu.VMEM((128, channels), jnp.float32),
        ],
        compiler_params=params(),
        cost_estimate=light(),
    )(first, across[0], shifted[1], across[1], taps)

    parts = terms(2 * rows, windows, grads, 2, 3)
    stay = [keep + other_core(send) for send, keep in zip(parts[:3], parts[3:])]
    total = jnp.concatenate(stay) * factor + crossed
    weight_grad = jnp.transpose(total.reshape(3, 3, 3, share, outputs), (3, 0, 1, 2, 4))
    return (grad_latents.reshape(latents.shape), weight_grad)


def from_behind(shard, axis, by):
    peers = lax.axis_size(axis)
    pairs = [(i, i + by) for i in range(peers) if 0 <= i + by < peers]
    return lax.ppermute(shard, axis, pairs)


def with_halo(block, sides, width):
    for axis, dim in sides:
        count = lax.axis_size(axis)
        forward = [(i, i + 1) for i in range(count - 1)]
        backward = [(target, source) for source, target in forward]
        low = lax.ppermute(
            lax.slice_in_dim(block, block.shape[dim] - width, None, axis=dim), axis, forward
        )
        high = lax.ppermute(lax.slice_in_dim(block, 0, width, axis=dim), axis, backward)
        block = jnp.concatenate([low, block, high], axis=dim)
    return block


def tap_terms(source, grad_flat, frames, height, width):
    taps = []
    for a in range(3):
        for i in range(3):
            for j in range(3):
                window = source[a : a + frames, i : i + height, j : j + width]
                flat = window.reshape(frames * height * width, window.shape[3])
                taps.append(
                    lax.dot_general(
                        flat,
                        grad_flat,
                        (((0,), (0,)), ((), ())),
                        preferred_element_type=jnp.float32,
                    )
                )
    return jnp.stack(taps, axis=1)


def wide_body(latents, grad_out, kernel):
    frames = grad_out.shape[1]
    height = grad_out.shape[2]
    width = grad_out.shape[3]
    channels = latents.shape[4]
    outputs = grad_out.shape[4]
    devices = lax.axis_size("dp") * lax.axis_size("tm") * lax.axis_size("rows")
    factor = float(devices * frames * height * width) ** (-0.5)
    earlier = from_behind(latents, "tm", 1)
    with_earlier = jnp.concatenate([earlier, latents], axis=1)
    grad_ext = with_halo(grad_out, (("rows", 2),), 1)
    later = from_behind(grad_ext, "tm", -1)
    grad_all = jnp.concatenate([grad_ext, later], axis=1)[0]
    grad_all = jnp.pad(grad_all, ((0, 0), (0, 0), (1, 1), (0, 0)))
    grad_up = jnp.zeros((frames, height, width, channels), jnp.float32)
    for a in range(3):
        for i in range(3):
            for j in range(3):
                window = grad_all[
                    2 - a : 2 - a + frames, 2 - i : 2 - i + height, 2 - j : 2 - j + width
                ]
                grad_up = grad_up + lax.dot_general(
                    window,
                    kernel[a, i, j],
                    (((3,), (1,)), ((), ())),
                    preferred_element_type=jnp.float32,
                )
    pooled = grad_up.reshape(frames, height // 2, 2, width // 2, 2, channels).sum(axis=(2, 4))
    grad_latents = pooled.astype(jnp.bfloat16)[None]
    slab_count = lax.axis_size("rows")
    groups = lax.axis_size("dp") * lax.axis_size("tm")
    share = channels // devices
    lead = with_earlier.shape[:4]
    regrouped = with_earlier.reshape(lead + (groups, slab_count, share))
    regrouped = jnp.swapaxes(regrouped, 4, 5).reshape(lead + (channels,))
    owned = lax.all_to_all(regrouped, "rows", split_axis=4, concat_axis=2, tiled=True)[0]
    source = jnp.repeat(jnp.repeat(owned, 2, axis=1), 2, axis=2)
    source = jnp.pad(source, ((0, 0), (1, 1), (1, 1), (0, 0)))
    grad_whole = lax.all_gather(grad_out, "rows", axis=2, tiled=True)[0]
    whole_height = grad_whole.shape[1]
    grad_flat = grad_whole.reshape(frames * whole_height * width, outputs)
    term = tap_terms(source, grad_flat, frames, whole_height, width) * factor
    term = term.reshape(source.shape[3], 3, 3, 3, outputs)
    weight_grad = lax.psum_scatter(term, ("dp", "tm"), scatter_dimension=0, tiled=True)
    return (grad_latents, weight_grad)


def body(latents, grad_out, kernel):
    share = latents.shape[4] // (lax.axis_size("dp") * lax.axis_size("tm") * lax.axis_size("rows"))
    narrow = lax.axis_size("rows") == 2 and lax.axis_size("dp") == 4 and lax.axis_size("tm") > 2 and share == 16
    return (narrow_body if narrow else wide_body)(latents, grad_out, kernel)


def solution(mesh):
    in_specs = (P("dp", "tm", "rows", None, None), P("dp", "tm", "rows", None, None), P())
    out_specs = (P("dp", "tm", "rows", None, None), P(("dp", "tm", "rows"), None, None, None, None))
    return jax.shard_map(body, mesh=mesh, in_specs=in_specs, out_specs=out_specs, check_vma=False)
```

```python
import functools

import jax
import jax.numpy as jnp
from jax import lax
from jax.experimental import pallas as pl
from jax.experimental.pallas import tpu as pltpu
from jax.sharding import PartitionSpec as P

VMEM_LIMIT = 40 * 1024 * 1024
SLOTS = (3, 2, 1, 0)


def cycle(size, by):
    return [(i, (i + by) % size) for i in range(size)]


def whole(count):
    return [pl.BlockSpec(memory_space=pltpu.VMEM)] * count


def params(limit=VMEM_LIMIT):
    return pltpu.CompilerParams(vmem_limit_bytes=limit)


def light():
    return pl.CostEstimate(flops=1, bytes_accessed=1, transcendentals=0)


LATENT_ROWS = 16
MESSAGE_ROWS = LATENT_ROWS + 120


def pick_kernel(tm, share, pick_ref):
    channels = pick_ref.shape[0]
    me_dp, me_tm, me_rows = lax.axis_index("dp"), lax.axis_index("tm"), lax.axis_index("rows")
    col = lax.broadcasted_iota(jnp.int32, (1, channels), 1)
    inner = col % share
    place = (col // share) % 4
    crossing = (col // (4 * share)) % 2
    shift = col // (8 * share)
    slot = jnp.where(place == 0, SLOTS[0], jnp.where(place == 1, SLOTS[1], jnp.where(place == 2, SLOTS[2], SLOTS[3])))
    dp = jnp.bitwise_xor(slot, me_dp)
    rows = jnp.bitwise_xor(crossing, me_rows)
    wanted = ((dp * tm + (shift + me_tm) % tm) * 2 + rows) * share + inner
    row = lax.broadcasted_iota(jnp.int32, (channels, channels), 0)
    pick_ref[...] = jnp.where(row == wanted, 1.0, 0.0).astype(jnp.bfloat16)


def message_kernel(tm, pick_ref, lat_ref, grad_ref, *refs):
    outs, wide_ref = refs[:tm], refs[tm]
    channels = pick_ref.shape[0]
    lat = lat_ref[...].reshape(60, channels)
    wide_ref[56:64, :] = jnp.zeros((8, channels), jnp.float32)
    wide_ref[0:60, :] = jnp.dot(lat, pick_ref[...], preferred_element_type=jnp.float32)
    grads = [grad_ref[f].reshape(120, grad_ref.shape[3]) for f in range(2)]
    for k in range(tm):
        for part in range(4):
            piece = wide_ref[16 * part : 16 * part + 16, 128 * k : 128 * k + 128].astype(jnp.bfloat16)
            lanes = slice(128 * (part % 2), 128 * (part % 2) + 128)
            outs[k][part // 2, 0:LATENT_ROWS, lanes] = piece
        for f in range(2):
            outs[k][f, LATENT_ROWS:, :] = grads[f]


def arrange_kernel(tm, share, shifts, late, *refs):
    blocks = refs[: 2 * len(shifts)]
    win_ref, grad_ref, pick_ref, lat_ref = refs[-4:]
    group = 4 * share
    me_tm, me_rows = lax.axis_index("tm"), lax.axis_index("rows")
    if 0 in shifts:
        kappa = lax.broadcasted_iota(jnp.int32, (128, 128), 0)
        rho = lax.broadcasted_iota(jnp.int32, (1, 128), 1)
        w, h = rho // 2, rho % 2
        for f in range(2):
            for ij in range(9):
                i, j = ij // 3, ij % 3
                for s in range(2):
                    r = (2 * s + h + 1 + i) // 2 - 1
                    q = (w + 1 + j) // 2 - 1
                    ok = (r >= 0) & (r < 2) & (q >= 0) & (q < 30) & (rho < 120)
                    target = jnp.where(ok, r * 64 + q * 2 + f, -1)
                    pick = jnp.where(kappa == target, 1.0, 0.0).astype(jnp.bfloat16)
                    base = (f * 9 + ij) * 256 + s * 128
                    pick_ref[:, base : base + 128] = pick
        win_ref[0:2] = jnp.zeros((2,) + win_ref.shape[1:], jnp.bfloat16)
        t = lax.rem(me_tm + tm - late, tm)
        win_ref[pl.ds(2 * t + 2, 2)] = jnp.zeros((2,) + win_ref.shape[1:], jnp.bfloat16)
        grad_ref[pl.ds(2 * t, 2)] = jnp.zeros((2,) + grad_ref.shape[1:], jnp.bfloat16)
    where = [lax.rem(me_tm + tm - k, tm) for k in shifts]
    for n, t in enumerate(where):
        for half, rows in enumerate((me_rows, 1 - me_rows)):
            block = blocks[2 * n + half]
            for part in range(4):
                lanes = slice(128 * (part % 2) + group * half, 128 * (part % 2) + group * (half + 1))
                piece = block[part // 2, 0:LATENT_ROWS, lanes]
                lat_ref[n, rows, 16 * part : 16 * part + 16, :] = piece.astype(jnp.float32)
            for f in range(2):
                grad_ref[2 * t + f, rows, 112:128, :] = jnp.zeros((16, grad_ref.shape[3]), jnp.bfloat16)
                grad_ref[2 * t + f, rows, 0:120, :] = block[f, LATENT_ROWS:, :]
    stacked = jnp.concatenate(
        [jnp.transpose(lat_ref[n].reshape(128, group)) for n in range(len(shifts))], axis=0
    ).astype(jnp.bfloat16)
    for f in range(2):
        for ij in range(9):
            base = (f * 9 + ij) * 256
            wide = jnp.dot(stacked, pick_ref[:, base : base + 256], preferred_element_type=jnp.float32)
            wide = wide.astype(jnp.bfloat16)
            for n, t in enumerate(where):
                for p in range(4):
                    src = n * group + p * share
                    dst = p * 9 * share + ij * share
                    win_ref[2 * t + f + 2, dst : dst + share, :] = wide[src : src + share]


def terms_kernel(first, taps, frames, outs, win_ref, grad_ref, *out_refs):
    each = len(out_refs) // outs
    rows = out_refs[0].shape[0] * each // len(taps)
    span = slice(first, first + rows * outs)
    total = None
    for f in range(frames):
        grad = grad_ref[f].reshape(256, grad_ref.shape[3])
        lhs = jnp.concatenate([win_ref[f + a, span, :] for a in taps], axis=0)
        term = jnp.dot(lhs, grad, preferred_element_type=jnp.float32)
        total = term if total is None else total + term
    for n in range(len(taps)):
        for m in range(outs):
            start = (n * outs + m) * rows
            ref = out_refs[m * each + n % each]
            place = n // each * rows
            ref[place : place + rows] = total[start : start + rows]


def late_terms(tm, late, first, win_ref, grad_ref, part_ref, out_ref):
    rows = part_ref.shape[0] // 3
    frames = grad_ref.shape[0]
    block = lax.rem(lax.axis_index("tm") + tm - late, tm)
    total = [part_ref[a * rows : (a + 1) * rows] for a in range(3)]
    for step, taps in enumerate(((0, 1, 2), (0, 1, 2), (0, 1), (0,))):
        frame = 2 * block + step
        if step > 1:
            inside = jnp.where(frame < frames, 1.0, 0.0).astype(jnp.bfloat16)
            frame = jnp.minimum(frame, frames - 1)
        grad = grad_ref[frame].reshape(256, grad_ref.shape[3])
        if step > 1:
            grad = grad * inside
        lhs = jnp.concatenate([win_ref[frame + a, first : first + rows, :] for a in taps], axis=0)
        term = jnp.dot(lhs, grad, preferred_element_type=jnp.float32)
        for n, a in enumerate(taps):
            total[a] = total[a] + term[n * rows : (n + 1) * rows]
    for a in range(3):
        out_ref[a * rows : (a + 1) * rows] = total[a]


def arrange_late_kernel(tm, share, late, own_ref, other_ref, w_ref, g_ref, p_ref, part_ref, *refs):
    win_ref, grad_ref, pick_ref, out_ref, lat_ref = refs
    arrange_kernel(tm, share, (late,), late, own_ref, other_ref, win_ref, grad_ref, pick_ref, lat_ref)
    late_terms(tm, late, 0, win_ref, grad_ref, part_ref, out_ref)


def keep_late_kernel(tm, late, win_ref, grad_ref, part_ref, out_ref):
    late_terms(tm, late, part_ref.shape[0] // 3, win_ref, grad_ref, part_ref, out_ref)


TOP_EXPONENT = 14
EXPONENT_ROWS = 16


def pack_kernel(keep_ref, received_ref, out_ref):
    rows = keep_ref.shape[0]
    total = keep_ref[...] + received_ref[...]
    top = jnp.max(jnp.max(jnp.abs(total), axis=0, keepdims=True), axis=1, keepdims=True)
    exponent = jnp.floor(jnp.log2(jnp.maximum(top, 2.0**-100))) - TOP_EXPONENT
    out_ref[0:rows] = total * jnp.exp2(-exponent)
    out_ref[rows:] = jnp.broadcast_to(exponent, (EXPONENT_ROWS, out_ref.shape[1]))


def latents_kernel(tm, own_ref, other_ref, next_ref, next_other_ref, kernel_ref, out_ref, wide_ref, pool_ref, total_ref):
    step = pl.program_id(0)
    outputs = own_ref.shape[2]

    @pl.when(step == 0)
    def _():
        me_tm, me_rows = lax.axis_index("tm"), lax.axis_index("rows")
        later = jnp.where(me_tm < tm - 1, 1.0, 0.0)
        above = jnp.where(me_rows > 0, 1.0, 0.0)
        lanes = outputs // 128
        wide_ref[:, :, 120:128, :] = jnp.zeros((2, lanes, 8, 128), jnp.float32)

        def every_fourth(source, first):
            parts = [wide_ref[source, n, pl.ds(first, 32, stride=4), :] for n in range(lanes)]
            return jnp.concatenate(parts, axis=1)

        for f in range(4):
            mine, theirs = (own_ref, other_ref) if f < 2 else (next_ref, next_other_ref)
            for n in range(lanes):
                wide_ref[0, n, 0:120, :] = mine[f % 2, LATENT_ROWS:, 128 * n : 128 * n + 128].astype(jnp.float32)
                wide_ref[1, n, 0:120, :] = theirs[f % 2, LATENT_ROWS:, 128 * n : 128 * n + 128].astype(jnp.float32)
            x = [[every_fourth(0, 2 * t + h) for t in range(2)] for h in range(2)]
            up = [every_fourth(1, 2 * t + 1) * above for t in range(2)]
            down = [every_fourth(1, 2 * t) * (1.0 - above) for t in range(2)]
            sums = (
                [x[1][t] + down[t] for t in range(2)],
                [x[0][t] + x[1][t] for t in range(2)],
                [up[t] + x[0][t] for t in range(2)],
            )
            for i in range(3):
                even, odd = sums[i]
                after = pltpu.roll(even, 31, 0)
                before = pltpu.roll(odd, 1, 0)
                for j, pooled in enumerate((odd + after, even + odd, before + even)):
                    if f >= 2:
                        pooled = pooled * later
                    high = pooled.astype(jnp.bfloat16)
                    low = (pooled - high.astype(jnp.float32)).astype(jnp.bfloat16)
                    pool_ref[3 * i + j, 0, f] = high
                    pool_ref[3 * i + j, 1, f] = low
        total_ref[...] = jnp.zeros_like(total_ref)

    total = total_ref[...]
    for ij in range(9):
        lhs = pool_ref[ij, :, pl.ds(2 - step, 2)].reshape(128, outputs)
        total = total + lax.dot_general(
            lhs, kernel_ref[ij], (((1,), (1,)), ((), ())), preferred_element_type=jnp.float32
        )
    total_ref[...] = total

    @pl.when(step == 2)
    def _():
        for f in range(2):
            sum_f = total[32 * f : 32 * f + 32] + total[64 + 32 * f : 96 + 32 * f]
            out_ref[f] = sum_f[0:30].astype(jnp.bfloat16)


def narrow_body(latents, grad_out, kernel):
    tm = lax.axis_size("tm")
    devices = lax.axis_size("dp") * tm * 2
    channels = latents.shape[4]
    outputs = grad_out.shape[4]
    share = channels // devices
    frames = 2 * tm
    factor = float(devices * 240) ** (-0.5)
    swap = [(0, 1), (1, 0)]

    mine = jnp.transpose(grad_out[0], (0, 2, 1, 3))
    lat = jnp.transpose(latents[0, :, 0], (1, 0, 2))
    message = jax.ShapeDtypeStruct((2, MESSAGE_ROWS, outputs), jnp.bfloat16)
    pick = pl.pallas_call(
        functools.partial(pick_kernel, tm, share),
        out_shape=jax.ShapeDtypeStruct((channels, channels), jnp.bfloat16),
        in_specs=[],
        out_specs=whole(1)[0],
        compiler_params=params(),
        cost_estimate=pl.CostEstimate(flops=2**33, bytes_accessed=2**24, transcendentals=0),
    )()
    messages = pl.pallas_call(
        functools.partial(message_kernel, tm),
        out_shape=tuple([message] * tm),
        in_specs=whole(3),
        out_specs=tuple(whole(tm)),
        scratch_shapes=[pltpu.VMEM((64, channels), jnp.float32)],
        compiler_params=params(),
    )(pick, lat, mine)
    order = [0, tm - 1] + list(range(1, tm - 1))
    shifted = [lax.ppermute(messages[k], "tm", cycle(tm, k)) if k else messages[0] for k in order]
    across = [lax.ppermute(block, "rows", swap) for block in shifted]

    arranged = (
        jax.ShapeDtypeStruct((frames + 2, 36 * share, 256), jnp.bfloat16),
        jax.ShapeDtypeStruct((frames, 2, 128, outputs), jnp.bfloat16),
        jax.ShapeDtypeStruct((128, 18 * 256), jnp.bfloat16),
    )

    late = order[-1]
    early = [block for pair in zip(shifted[:-1], across[:-1]) for block in pair]
    early = pl.pallas_call(
        functools.partial(arrange_kernel, tm, share, tuple(order[:-1]), late),
        out_shape=arranged,
        in_specs=whole(len(early)),
        out_specs=tuple(whole(3)),
        scratch_shapes=[pltpu.VMEM((tm - 1, 2, 64, 4 * share), jnp.float32)],
        compiler_params=params(),
        cost_estimate=light(),
    )(*early)

    rows = 9 * share

    def terms(first, windows, grads, outs, each):
        out = jax.ShapeDtypeStruct((3 // each * rows, outputs), jnp.float32)
        return pl.pallas_call(
            functools.partial(terms_kernel, first, (0, 1, 2), frames, outs),
            out_shape=tuple([out] * (outs * each)),
            in_specs=whole(2),
            out_specs=tuple(whole(outs * each)),
            compiler_params=params(),
            cost_estimate=light(),
        )(windows, grads)

    def other_core(block):
        return lax.ppermute(block, "dp", [(i, i ^ 1) for i in range(4)])

    send, keep = terms(0, early[0], early[1], 2, 1)
    windows, grads, _, send = pl.pallas_call(
        functools.partial(arrange_late_kernel, tm, share, late),
        out_shape=arranged + (jax.ShapeDtypeStruct(send.shape, jnp.float32),),
        in_specs=whole(6),
        out_specs=tuple(whole(4)),
        scratch_shapes=[pltpu.VMEM((1, 2, 64, 4 * share), jnp.float32)],
        input_output_aliases={2: 0, 3: 1, 4: 2},
        compiler_params=params(),
        cost_estimate=light(),
    )(shifted[-1], across[-1], *early, send)
    keep = pl.pallas_call(
        functools.partial(keep_late_kernel, tm, late),
        out_shape=jax.ShapeDtypeStruct(keep.shape, jnp.float32),
        in_specs=whole(3),
        out_specs=whole(1)[0],
        compiler_params=params(),
        cost_estimate=light(),
    )(windows, grads, keep)
    chip = pl.pallas_call(
        pack_kernel,
        out_shape=jax.ShapeDtypeStruct((3 * rows + EXPONENT_ROWS, outputs), jnp.float32),
        in_specs=whole(2),
        out_specs=whole(1)[0],
        compiler_params=params(),
        cost_estimate=light(),
    )(keep, other_core(send))
    chip = chip.astype(jnp.float16)
    crossed = lax.ppermute(chip, "dp", [(i, i ^ 2) for i in range(4)]).astype(jnp.float32)
    crossed = crossed[: 3 * rows] * (jnp.exp2(crossed[3 * rows : 3 * rows + 1]) * factor)
    windows, first, *_ = lax.optimization_barrier((windows, shifted[0], chip))
    taps = kernel.reshape(27, channels, outputs)
    grad_latents = pl.pallas_call(
        functools.partial(latents_kernel, tm),
        grid=(3,),
        out_shape=jax.ShapeDtypeStruct((2, 30, channels), jnp.bfloat16),
        in_specs=[pl.BlockSpec((2, MESSAGE_ROWS, outputs), lambda a: (0, 0, 0))] * 4
        + [pl.BlockSpec((9, channels, outputs), lambda a: (a, 0, 0))],
        out_specs=pl.BlockSpec((2, 30, channels), lambda a: (0, 0, 0)),
        scratch_shapes=[
            pltpu.VMEM((2, outputs // 128, 128, 128), jnp.float32),
            pltpu.VMEM((9, 2, 4, 32, outputs), jnp.bfloat16),
            pltpu.VMEM((128, channels), jnp.float32),
        ],
        compiler_params=params(),
        cost_estimate=light(),
    )(first, across[0], shifted[1], across[1], taps)

    parts = terms(2 * rows, windows, grads, 2, 3)
    stay = [keep + other_core(send) for send, keep in zip(parts[:3], parts[3:])]
    total = jnp.concatenate(stay) * factor + crossed
    weight_grad = jnp.transpose(total.reshape(3, 3, 3, share, outputs), (3, 0, 1, 2, 4))
    return (grad_latents.reshape(latents.shape), weight_grad)


def from_behind(shard, axis, by):
    peers = lax.axis_size(axis)
    pairs = [(i, i + by) for i in range(peers) if 0 <= i + by < peers]
    return lax.ppermute(shard, axis, pairs)


def with_halo(block, sides, width):
    for axis, dim in sides:
        count = lax.axis_size(axis)
        forward = [(i, i + 1) for i in range(count - 1)]
        backward = [(target, source) for source, target in forward]
        low = lax.ppermute(
            lax.slice_in_dim(block, block.shape[dim] - width, None, axis=dim), axis, forward
        )
        high = lax.ppermute(lax.slice_in_dim(block, 0, width, axis=dim), axis, backward)
        block = jnp.concatenate([low, block, high], axis=dim)
    return block


def tap_terms(source, grad_flat, frames, height, width):
    taps = []
    for a in range(3):
        for i in range(3):
            for j in range(3):
                window = source[a : a + frames, i : i + height, j : j + width]
                flat = window.reshape(frames * height * width, window.shape[3])
                taps.append(
                    lax.dot_general(
                        flat,
                        grad_flat,
                        (((0,), (0,)), ((), ())),
                        preferred_element_type=jnp.float32,
                    )
                )
    return jnp.stack(taps, axis=1)


def wide_body(latents, grad_out, kernel):
    frames = grad_out.shape[1]
    height = grad_out.shape[2]
    width = grad_out.shape[3]
    channels = latents.shape[4]
    outputs = grad_out.shape[4]
    devices = lax.axis_size("dp") * lax.axis_size("tm") * lax.axis_size("rows")
    factor = float(devices * frames * height * width) ** (-0.5)
    earlier = from_behind(latents, "tm", 1)
    with_earlier = jnp.concatenate([earlier, latents], axis=1)
    grad_ext = with_halo(grad_out, (("rows", 2),), 1)
    later = from_behind(grad_ext, "tm", -1)
    grad_all = jnp.concatenate([grad_ext, later], axis=1)[0]
    grad_all = jnp.pad(grad_all, ((0, 0), (0, 0), (1, 1), (0, 0)))
    grad_up = jnp.zeros((frames, height, width, channels), jnp.float32)
    for a in range(3):
        for i in range(3):
            for j in range(3):
                window = grad_all[
                    2 - a : 2 - a + frames, 2 - i : 2 - i + height, 2 - j : 2 - j + width
                ]
                grad_up = grad_up + lax.dot_general(
                    window,
                    kernel[a, i, j],
                    (((3,), (1,)), ((), ())),
                    preferred_element_type=jnp.float32,
                )
    pooled = grad_up.reshape(frames, height // 2, 2, width // 2, 2, channels).sum(axis=(2, 4))
    grad_latents = pooled.astype(jnp.bfloat16)[None]
    slab_count = lax.axis_size("rows")
    groups = lax.axis_size("dp") * lax.axis_size("tm")
    share = channels // devices
    lead = with_earlier.shape[:4]
    regrouped = with_earlier.reshape(lead + (groups, slab_count, share))
    regrouped = jnp.swapaxes(regrouped, 4, 5).reshape(lead + (channels,))
    owned = lax.all_to_all(regrouped, "rows", split_axis=4, concat_axis=2, tiled=True)[0]
    source = jnp.repeat(jnp.repeat(owned, 2, axis=1), 2, axis=2)
    source = jnp.pad(source, ((0, 0), (1, 1), (1, 1), (0, 0)))
    grad_whole = lax.all_gather(grad_out, "rows", axis=2, tiled=True)[0]
    whole_height = grad_whole.shape[1]
    grad_flat = grad_whole.reshape(frames * whole_height * width, outputs)
    term = tap_terms(source, grad_flat, frames, whole_height, width) * factor
    term = term.reshape(source.shape[3], 3, 3, 3, outputs)
    weight_grad = lax.psum_scatter(term, ("dp", "tm"), scatter_dimension=0, tiled=True)
    return (grad_latents, weight_grad)


def body(latents, grad_out, kernel):
    share = latents.shape[4] // (lax.axis_size("dp") * lax.axis_size("tm") * lax.axis_size("rows"))
    narrow = lax.axis_size("rows") == 2 and lax.axis_size("dp") == 4 and lax.axis_size("tm") > 2 and share == 16
    return (narrow_body if narrow else wide_body)(latents, grad_out, kernel)


def solution(mesh):
    in_specs = (P("dp", "tm", "rows", None, None), P("dp", "tm", "rows", None, None), P())
    out_specs = (P("dp", "tm", "rows", None, None), P(("dp", "tm", "rows"), None, None, None, None))
    return jax.shard_map(body, mesh=mesh, in_specs=in_specs, out_specs=out_specs, check_vma=False)
```

```python
import functools

import jax
import jax.numpy as jnp
from jax import lax
from jax.experimental import pallas as pl
from jax.experimental.pallas import tpu as pltpu
from jax.sharding import PartitionSpec as P

VMEM_LIMIT = 40 * 1024 * 1024
SLOTS = (3, 2, 1, 0)


def cycle(size, by):
    return [(i, (i + by) % size) for i in range(size)]


def whole(count):
    return [pl.BlockSpec(memory_space=pltpu.VMEM)] * count


def params(limit=VMEM_LIMIT):
    return pltpu.CompilerParams(vmem_limit_bytes=limit)


def light():
    return pl.CostEstimate(flops=1, bytes_accessed=1, transcendentals=0)


LATENT_ROWS = 16
MESSAGE_ROWS = LATENT_ROWS + 120


def pick_kernel(tm, share, pick_ref):
    channels = pick_ref.shape[0]
    me_dp, me_tm, me_rows = lax.axis_index("dp"), lax.axis_index("tm"), lax.axis_index("rows")
    col = lax.broadcasted_iota(jnp.int32, (1, channels), 1)
    inner = col % share
    place = (col // share) % 4
    crossing = (col // (4 * share)) % 2
    shift = col // (8 * share)
    slot = jnp.where(place == 0, SLOTS[0], jnp.where(place == 1, SLOTS[1], jnp.where(place == 2, SLOTS[2], SLOTS[3])))
    dp = jnp.bitwise_xor(slot, me_dp)
    rows = jnp.bitwise_xor(crossing, me_rows)
    wanted = ((dp * tm + (shift + me_tm) % tm) * 2 + rows) * share + inner
    row = lax.broadcasted_iota(jnp.int32, (channels, channels), 0)
    pick_ref[...] = jnp.where(row == wanted, 1.0, 0.0).astype(jnp.bfloat16)


def message_kernel(tm, pick_ref, lat_ref, grad_ref, *refs):
    outs, wide_ref = refs[:tm], refs[tm]
    channels = pick_ref.shape[0]
    lat = lat_ref[...].reshape(60, channels)
    wide_ref[56:64, :] = jnp.zeros((8, channels), jnp.float32)
    wide_ref[0:60, :] = jnp.dot(lat, pick_ref[...], preferred_element_type=jnp.float32)
    grads = [grad_ref[f].reshape(120, grad_ref.shape[3]) for f in range(2)]
    for k in range(tm):
        for part in range(4):
            piece = wide_ref[16 * part : 16 * part + 16, 128 * k : 128 * k + 128].astype(jnp.bfloat16)
            lanes = slice(128 * (part % 2), 128 * (part % 2) + 128)
            outs[k][part // 2, 0:LATENT_ROWS, lanes] = piece
        for f in range(2):
            outs[k][f, LATENT_ROWS:, :] = grads[f]


def arrange_kernel(tm, share, shifts, late, *refs):
    blocks = refs[: 2 * len(shifts)]
    win_ref, grad_ref, pick_ref, lat_ref = refs[-4:]
    group = 4 * share
    me_tm, me_rows = lax.axis_index("tm"), lax.axis_index("rows")
    if 0 in shifts:
        kappa = lax.broadcasted_iota(jnp.int32, (128, 128), 0)
        rho = lax.broadcasted_iota(jnp.int32, (1, 128), 1)
        w, h = rho // 2, rho % 2
        for f in range(2):
            for ij in range(9):
                i, j = ij // 3, ij % 3
                for s in range(2):
                    r = (2 * s + h + 1 + i) // 2 - 1
                    q = (w + 1 + j) // 2 - 1
                    ok = (r >= 0) & (r < 2) & (q >= 0) & (q < 30) & (rho < 120)
                    target = jnp.where(ok, r * 64 + q * 2 + f, -1)
                    pick = jnp.where(kappa == target, 1.0, 0.0).astype(jnp.bfloat16)
                    base = (f * 9 + ij) * 256 + s * 128
                    pick_ref[:, base : base + 128] = pick
        win_ref[0:2] = jnp.zeros((2,) + win_ref.shape[1:], jnp.bfloat16)
        t = lax.rem(me_tm + tm - late, tm)
        win_ref[pl.ds(2 * t + 2, 2)] = jnp.zeros((2,) + win_ref.shape[1:], jnp.bfloat16)
        grad_ref[pl.ds(2 * t, 2)] = jnp.zeros((2,) + grad_ref.shape[1:], jnp.bfloat16)
    where = [lax.rem(me_tm + tm - k, tm) for k in shifts]
    for n, t in enumerate(where):
        for half, rows in enumerate((me_rows, 1 - me_rows)):
            block = blocks[2 * n + half]
            for part in range(4):
                lanes = slice(128 * (part % 2) + group * half, 128 * (part % 2) + group * (half + 1))
                piece = block[part // 2, 0:LATENT_ROWS, lanes]
                lat_ref[n, rows, 16 * part : 16 * part + 16, :] = piece.astype(jnp.float32)
            for f in range(2):
                grad_ref[2 * t + f, rows, 112:128, :] = jnp.zeros((16, grad_ref.shape[3]), jnp.bfloat16)
                grad_ref[2 * t + f, rows, 0:120, :] = block[f, LATENT_ROWS:, :]
    stacked = jnp.concatenate(
        [jnp.transpose(lat_ref[n].reshape(128, group)) for n in range(len(shifts))], axis=0
    ).astype(jnp.bfloat16)
    for f in range(2):
        for ij in range(9):
            base = (f * 9 + ij) * 256
            wide = jnp.dot(stacked, pick_ref[:, base : base + 256], preferred_element_type=jnp.float32)
            wide = wide.astype(jnp.bfloat16)
            for n, t in enumerate(where):
                for p in range(4):
                    src = n * group + p * share
                    dst = p * 9 * share + ij * share
                    win_ref[2 * t + f + 2, dst : dst + share, :] = wide[src : src + share]


def terms_kernel(first, taps, frames, outs, win_ref, grad_ref, *out_refs):
    each = len(out_refs) // outs
    rows = out_refs[0].shape[0] * each // len(taps)
    span = slice(first, first + rows * outs)
    total = None
    for f in range(frames):
        grad = grad_ref[f].reshape(256, grad_ref.shape[3])
        lhs = jnp.concatenate([win_ref[f + a, span, :] for a in taps], axis=0)
        term = jnp.dot(lhs, grad, preferred_element_type=jnp.float32)
        total = term if total is None else total + term
    for n in range(len(taps)):
        for m in range(outs):
            start = (n * outs + m) * rows
            ref = out_refs[m * each + n % each]
            place = n // each * rows
            ref[place : place + rows] = total[start : start + rows]


def late_terms(tm, late, first, win_ref, grad_ref, part_ref, out_ref):
    rows = part_ref.shape[0] // 3
    frames = grad_ref.shape[0]
    block = lax.rem(lax.axis_index("tm") + tm - late, tm)
    total = [part_ref[a * rows : (a + 1) * rows] for a in range(3)]
    for step, taps in enumerate(((0, 1, 2), (0, 1, 2), (0, 1), (0,))):
        frame = 2 * block + step
        if step > 1:
            inside = jnp.where(frame < frames, 1.0, 0.0).astype(jnp.bfloat16)
            frame = jnp.minimum(frame, frames - 1)
        grad = grad_ref[frame].reshape(256, grad_ref.shape[3])
        if step > 1:
            grad = grad * inside
        lhs = jnp.concatenate([win_ref[frame + a, first : first + rows, :] for a in taps], axis=0)
        term = jnp.dot(lhs, grad, preferred_element_type=jnp.float32)
        for n, a in enumerate(taps):
            total[a] = total[a] + term[n * rows : (n + 1) * rows]
    for a in range(3):
        out_ref[a * rows : (a + 1) * rows] = total[a]


def arrange_late_kernel(tm, share, late, own_ref, other_ref, w_ref, g_ref, p_ref, part_ref, *refs):
    win_ref, grad_ref, pick_ref, out_ref, lat_ref = refs
    arrange_kernel(tm, share, (late,), late, own_ref, other_ref, win_ref, grad_ref, pick_ref, lat_ref)
    late_terms(tm, late, 0, win_ref, grad_ref, part_ref, out_ref)


def keep_late_kernel(tm, late, win_ref, grad_ref, part_ref, out_ref):
    late_terms(tm, late, part_ref.shape[0] // 3, win_ref, grad_ref, part_ref, out_ref)


TOP_EXPONENT = 14
EXPONENT_ROWS = 8


def pack_kernel(keep_ref, received_ref, out_ref):
    rows = keep_ref.shape[0]
    total = keep_ref[...] + received_ref[...]
    top = jnp.max(jnp.max(jnp.abs(total), axis=0, keepdims=True), axis=1, keepdims=True)
    exponent = jnp.floor(jnp.log2(jnp.maximum(top, 2.0**-100))) - TOP_EXPONENT
    out_ref[0:rows] = total * jnp.exp2(-exponent)
    out_ref[rows:] = jnp.broadcast_to(exponent, (EXPONENT_ROWS, out_ref.shape[1]))


def latents_kernel(tm, own_ref, other_ref, next_ref, next_other_ref, kernel_ref, out_ref, wide_ref, pool_ref, total_ref):
    step = pl.program_id(0)
    outputs = own_ref.shape[2]

    @pl.when(step == 0)
    def _():
        me_tm, me_rows = lax.axis_index("tm"), lax.axis_index("rows")
        later = jnp.where(me_tm < tm - 1, 1.0, 0.0)
        above = jnp.where(me_rows > 0, 1.0, 0.0)
        lanes = outputs // 128
        wide_ref[:, :, 120:128, :] = jnp.zeros((2, lanes, 8, 128), jnp.float32)

        def every_fourth(source, first):
            parts = [wide_ref[source, n, pl.ds(first, 32, stride=4), :] for n in range(lanes)]
            return jnp.concatenate(parts, axis=1)

        for f in range(4):
            mine, theirs = (own_ref, other_ref) if f < 2 else (next_ref, next_other_ref)
            for n in range(lanes):
                wide_ref[0, n, 0:120, :] = mine[f % 2, LATENT_ROWS:, 128 * n : 128 * n + 128].astype(jnp.float32)
                wide_ref[1, n, 0:120, :] = theirs[f % 2, LATENT_ROWS:, 128 * n : 128 * n + 128].astype(jnp.float32)
            x = [[every_fourth(0, 2 * t + h) for t in range(2)] for h in range(2)]
            up = [every_fourth(1, 2 * t + 1) * above for t in range(2)]
            down = [every_fourth(1, 2 * t) * (1.0 - above) for t in range(2)]
            sums = (
                [x[1][t] + down[t] for t in range(2)],
                [x[0][t] + x[1][t] for t in range(2)],
                [up[t] + x[0][t] for t in range(2)],
            )
            for i in range(3):
                even, odd = sums[i]
                after = pltpu.roll(even, 31, 0)
                before = pltpu.roll(odd, 1, 0)
                for j, pooled in enumerate((odd + after, even + odd, before + even)):
                    if f >= 2:
                        pooled = pooled * later
                    high = pooled.astype(jnp.bfloat16)
                    low = (pooled - high.astype(jnp.float32)).astype(jnp.bfloat16)
                    pool_ref[3 * i + j, 0, f] = high
                    pool_ref[3 * i + j, 1, f] = low
        total_ref[...] = jnp.zeros_like(total_ref)

    total = total_ref[...]
    for ij in range(9):
        lhs = pool_ref[ij, :, pl.ds(2 - step, 2)].reshape(128, outputs)
        total = total + lax.dot_general(
            lhs, kernel_ref[ij], (((1,), (1,)), ((), ())), preferred_element_type=jnp.float32
        )
    total_ref[...] = total

    @pl.when(step == 2)
    def _():
        for f in range(2):
            sum_f = total[32 * f : 32 * f + 32] + total[64 + 32 * f : 96 + 32 * f]
            out_ref[f] = sum_f[0:30].astype(jnp.bfloat16)


def narrow_body(latents, grad_out, kernel):
    tm = lax.axis_size("tm")
    devices = lax.axis_size("dp") * tm * 2
    channels = latents.shape[4]
    outputs = grad_out.shape[4]
    share = channels // devices
    frames = 2 * tm
    factor = float(devices * 240) ** (-0.5)
    swap = [(0, 1), (1, 0)]

    mine = jnp.transpose(grad_out[0], (0, 2, 1, 3))
    lat = jnp.transpose(latents[0, :, 0], (1, 0, 2))
    message = jax.ShapeDtypeStruct((2, MESSAGE_ROWS, outputs), jnp.bfloat16)
    pick = pl.pallas_call(
        functools.partial(pick_kernel, tm, share),
        out_shape=jax.ShapeDtypeStruct((channels, channels), jnp.bfloat16),
        in_specs=[],
        out_specs=whole(1)[0],
        compiler_params=params(),
        cost_estimate=pl.CostEstimate(flops=2**33, bytes_accessed=2**24, transcendentals=0),
    )()
    messages = pl.pallas_call(
        functools.partial(message_kernel, tm),
        out_shape=tuple([message] * tm),
        in_specs=whole(3),
        out_specs=tuple(whole(tm)),
        scratch_shapes=[pltpu.VMEM((64, channels), jnp.float32)],
        compiler_params=params(),
    )(pick, lat, mine)
    order = [0, tm - 1] + list(range(1, tm - 1))
    shifted = [lax.ppermute(messages[k], "tm", cycle(tm, k)) if k else messages[0] for k in order]
    across = [lax.ppermute(block, "rows", swap) for block in shifted]

    arranged = (
        jax.ShapeDtypeStruct((frames + 2, 36 * share, 256), jnp.bfloat16),
        jax.ShapeDtypeStruct((frames, 2, 128, outputs), jnp.bfloat16),
        jax.ShapeDtypeStruct((128, 18 * 256), jnp.bfloat16),
    )

    late = order[-1]
    early = [block for pair in zip(shifted[:-1], across[:-1]) for block in pair]
    early = pl.pallas_call(
        functools.partial(arrange_kernel, tm, share, tuple(order[:-1]), late),
        out_shape=arranged,
        in_specs=whole(len(early)),
        out_specs=tuple(whole(3)),
        scratch_shapes=[pltpu.VMEM((tm - 1, 2, 64, 4 * share), jnp.float32)],
        compiler_params=params(),
        cost_estimate=light(),
    )(*early)

    rows = 9 * share

    def terms(first, windows, grads, outs, each):
        out = jax.ShapeDtypeStruct((3 // each * rows, outputs), jnp.float32)
        return pl.pallas_call(
            functools.partial(terms_kernel, first, (0, 1, 2), frames, outs),
            out_shape=tuple([out] * (outs * each)),
            in_specs=whole(2),
            out_specs=tuple(whole(outs * each)),
            compiler_params=params(),
            cost_estimate=light(),
        )(windows, grads)

    def other_core(block):
        return lax.ppermute(block, "dp", [(i, i ^ 1) for i in range(4)])

    send, keep = terms(0, early[0], early[1], 2, 1)
    windows, grads, _, send = pl.pallas_call(
        functools.partial(arrange_late_kernel, tm, share, late),
        out_shape=arranged + (jax.ShapeDtypeStruct(send.shape, jnp.float32),),
        in_specs=whole(6),
        out_specs=tuple(whole(4)),
        scratch_shapes=[pltpu.VMEM((1, 2, 64, 4 * share), jnp.float32)],
        input_output_aliases={2: 0, 3: 1, 4: 2},
        compiler_params=params(),
        cost_estimate=light(),
    )(shifted[-1], across[-1], *early, send)
    keep = pl.pallas_call(
        functools.partial(keep_late_kernel, tm, late),
        out_shape=jax.ShapeDtypeStruct(keep.shape, jnp.float32),
        in_specs=whole(3),
        out_specs=whole(1)[0],
        compiler_params=params(),
        cost_estimate=light(),
    )(windows, grads, keep)
    chip = pl.pallas_call(
        pack_kernel,
        out_shape=jax.ShapeDtypeStruct((3 * rows + EXPONENT_ROWS, outputs), jnp.float32),
        in_specs=whole(2),
        out_specs=whole(1)[0],
        compiler_params=params(),
        cost_estimate=light(),
    )(keep, other_core(send))
    chip = chip.astype(jnp.float16)
    crossed = lax.ppermute(chip, "dp", [(i, i ^ 2) for i in range(4)]).astype(jnp.float32)
    crossed = crossed[: 3 * rows] * (jnp.exp2(crossed[3 * rows : 3 * rows + 1]) * factor)
    windows, first, *_ = lax.optimization_barrier((windows, shifted[0], chip))
    taps = kernel.reshape(27, channels, outputs)
    grad_latents = pl.pallas_call(
        functools.partial(latents_kernel, tm),
        grid=(3,),
        out_shape=jax.ShapeDtypeStruct((2, 30, channels), jnp.bfloat16),
        in_specs=[pl.BlockSpec((2, MESSAGE_ROWS, outputs), lambda a: (0, 0, 0))] * 4
        + [pl.BlockSpec((9, channels, outputs), lambda a: (a, 0, 0))],
        out_specs=pl.BlockSpec((2, 30, channels), lambda a: (0, 0, 0)),
        scratch_shapes=[
            pltpu.VMEM((2, outputs // 128, 128, 128), jnp.float32),
            pltpu.VMEM((9, 2, 4, 32, outputs), jnp.bfloat16),
            pltpu.VMEM((128, channels), jnp.float32),
        ],
        compiler_params=params(),
        cost_estimate=light(),
    )(first, across[0], shifted[1], across[1], taps)

    parts = terms(2 * rows, windows, grads, 2, 3)
    stay = [keep + other_core(send) for send, keep in zip(parts[:3], parts[3:])]
    total = jnp.concatenate(stay) * factor + crossed
    weight_grad = jnp.transpose(total.reshape(3, 3, 3, share, outputs), (3, 0, 1, 2, 4))
    return (grad_latents.reshape(latents.shape), weight_grad)


def from_behind(shard, axis, by):
    peers = lax.axis_size(axis)
    pairs = [(i, i + by) for i in range(peers) if 0 <= i + by < peers]
    return lax.ppermute(shard, axis, pairs)


def with_halo(block, sides, width):
    for axis, dim in sides:
        count = lax.axis_size(axis)
        forward = [(i, i + 1) for i in range(count - 1)]
        backward = [(target, source) for source, target in forward]
        low = lax.ppermute(
            lax.slice_in_dim(block, block.shape[dim] - width, None, axis=dim), axis, forward
        )
        high = lax.ppermute(lax.slice_in_dim(block, 0, width, axis=dim), axis, backward)
        block = jnp.concatenate([low, block, high], axis=dim)
    return block


def tap_terms(source, grad_flat, frames, height, width):
    taps = []
    for a in range(3):
        for i in range(3):
            for j in range(3):
                window = source[a : a + frames, i : i + height, j : j + width]
                flat = window.reshape(frames * height * width, window.shape[3])
                taps.append(
                    lax.dot_general(
                        flat,
                        grad_flat,
                        (((0,), (0,)), ((), ())),
                        preferred_element_type=jnp.float32,
                    )
                )
    return jnp.stack(taps, axis=1)


def wide_body(latents, grad_out, kernel):
    frames = grad_out.shape[1]
    height = grad_out.shape[2]
    width = grad_out.shape[3]
    channels = latents.shape[4]
    outputs = grad_out.shape[4]
    devices = lax.axis_size("dp") * lax.axis_size("tm") * lax.axis_size("rows")
    factor = float(devices * frames * height * width) ** (-0.5)
    earlier = from_behind(latents, "tm", 1)
    with_earlier = jnp.concatenate([earlier, latents], axis=1)
    grad_ext = with_halo(grad_out, (("rows", 2),), 1)
    later = from_behind(grad_ext, "tm", -1)
    grad_all = jnp.concatenate([grad_ext, later], axis=1)[0]
    grad_all = jnp.pad(grad_all, ((0, 0), (0, 0), (1, 1), (0, 0)))
    grad_up = jnp.zeros((frames, height, width, channels), jnp.float32)
    for a in range(3):
        for i in range(3):
            for j in range(3):
                window = grad_all[
                    2 - a : 2 - a + frames, 2 - i : 2 - i + height, 2 - j : 2 - j + width
                ]
                grad_up = grad_up + lax.dot_general(
                    window,
                    kernel[a, i, j],
                    (((3,), (1,)), ((), ())),
                    preferred_element_type=jnp.float32,
                )
    pooled = grad_up.reshape(frames, height // 2, 2, width // 2, 2, channels).sum(axis=(2, 4))
    grad_latents = pooled.astype(jnp.bfloat16)[None]
    slab_count = lax.axis_size("rows")
    groups = lax.axis_size("dp") * lax.axis_size("tm")
    share = channels // devices
    lead = with_earlier.shape[:4]
    regrouped = with_earlier.reshape(lead + (groups, slab_count, share))
    regrouped = jnp.swapaxes(regrouped, 4, 5).reshape(lead + (channels,))
    owned = lax.all_to_all(regrouped, "rows", split_axis=4, concat_axis=2, tiled=True)[0]
    source = jnp.repeat(jnp.repeat(owned, 2, axis=1), 2, axis=2)
    source = jnp.pad(source, ((0, 0), (1, 1), (1, 1), (0, 0)))
    grad_whole = lax.all_gather(grad_out, "rows", axis=2, tiled=True)[0]
    whole_height = grad_whole.shape[1]
    grad_flat = grad_whole.reshape(frames * whole_height * width, outputs)
    term = tap_terms(source, grad_flat, frames, whole_height, width) * factor
    term = term.reshape(source.shape[3], 3, 3, 3, outputs)
    weight_grad = lax.psum_scatter(term, ("dp", "tm"), scatter_dimension=0, tiled=True)
    return (grad_latents, weight_grad)


def body(latents, grad_out, kernel):
    share = latents.shape[4] // (lax.axis_size("dp") * lax.axis_size("tm") * lax.axis_size("rows"))
    narrow = lax.axis_size("rows") == 2 and lax.axis_size("dp") == 4 and lax.axis_size("tm") > 2 and share == 16
    return (narrow_body if narrow else wide_body)(latents, grad_out, kernel)


def solution(mesh):
    in_specs = (P("dp", "tm", "rows", None, None), P("dp", "tm", "rows", None, None), P())
    out_specs = (P("dp", "tm", "rows", None, None), P(("dp", "tm", "rows"), None, None, None, None))
    return jax.shard_map(body, mesh=mesh, in_specs=in_specs, out_specs=out_specs, check_vma=False)
```
